128 devices in a mesh: lat: 8 (over x, core), lon: 16 (over z, y).
Axes of the slice: x: 4, y: 4, z: 4, core: 2. Of those that a mesh axis runs over, the one named last changes fastest.
Arguments:
- fields: bfloat16 [720, 1440, 256], P('lat', 'lon'), may hold values from -6 to 6
- spectral_gain: float32 [720, 2, 256], replicated, may hold values from -6 to 6
- mix_weight: bfloat16 [2, 256, 256], replicated, may hold values from -0.25 to 0.25
- column_list: int32 [720], replicated, may hold values from 0 to 719, each once
- column_counts: int32 [128], replicated, may hold values from 1 to 7, 720 in all
Outputs:
- blended: bfloat16 [720, 1440, 256], P('lat', 'lon')
- spectrum: bfloat16 [128, 7, 720, 2, 256], P(('lat', 'lon'))
The draws below stay inside these ranges and needn't reach their ends.
Inputs may be any that keep to these rules, and one draw needn't show every extreme that they name: `column_list`: a permutation of the 720 orders. `column_counts`: the counts sum to 720; the largest is exactly 7.
All inputs are finite; a program needn't handle non-finite values.
Results may differ from the reference program's by a relative error of at most 0.012.
Values may be sent and summed in bfloat16 or wider, within the bound.
No kernel may reach another device: no remote copies, remote signals or barrier semaphores. Data moves between devices by JAX's collectives and lax.ppermute only.
A program may use at most 192 MiB of HBM per device.

```python
import math
import jax
import jax.numpy as jnp
import numpy as np
from jax import lax

NLAT = 720
NLON = 1440
C = 256
L = 720
M = 720
OWNERS = 128
CAP = 7
N_LAT = 8


def steps_of(stream_key, dims, shards, least, top_value):
    factor_of = 1.0
    for axis_at, shards_of in shards:
        steps = jax.random.uniform(jax.random.fold_in(jax.random.fold_in(stream_key, 6), axis_at), (shards_of,), jnp.float32, least / len(shards), top_value / len(shards))
        factor_of = factor_of * jnp.repeat(jnp.exp(steps), dims[axis_at] // shards_of).reshape((-1,) + (1,) * (len(dims) - 1 - axis_at))
    return factor_of


def profile(amount, total, most, slope):
    loads = [(1 << 20) // math.isqrt(rank ** slope) + 1 for rank in range(2, amount + 1)]
    rest, counts = total - most - (amount - 1), [1] * (amount - 1)
    while rest > 0:
        free = [i for i in range(amount - 1) if counts[i] < most]
        pool, left = sum([loads[i] for i in free]), rest
        for i in free:
            addition = min(most - counts[i], max(1, left * loads[i] // pool), rest)
            counts[i] = counts[i] + addition
            rest = rest - addition
    return np.array([most] + counts)


def ragged(rng, count, total, limit, lean):
    if count == 2:
        one = jax.random.randint(rng, (), max(1, total - limit), min(limit, total - 1) + 1)
        return jnp.stack([one, total - one])
    lengths = jnp.asarray(profile(count, total, limit, lean), jnp.int32)
    twos = (count - 1) // 2
    donor, receiver = lengths[1:1 + 2 * twos:2], lengths[2:2 + 2 * twos:2]
    room = jnp.minimum(donor - 1, limit - receiver)
    moved = jax.random.randint(jax.random.fold_in(rng, 1), (twos,), 0, 1 << 20) % (room + 1)
    lengths = lengths.at[1:1 + 2 * twos:2].set(donor - moved).at[2:2 + 2 * twos:2].set(receiver + moved)
    return lengths[jax.random.permutation(jax.random.fold_in(rng, 2), count)]


def normal_values(rng, shape, deviation, limit, split=(), kind=jnp.bfloat16):
    array = deviation * jax.random.normal(rng, shape, jnp.float32)
    if split:
        array = array * steps_of(rng, shape, split, -0.22, 0.18)
    return jnp.clip(array, -limit, limit).astype(kind)


def setup_inputs(seed: int = 0) -> dict:
    key_list = jax.random.split(jax.random.key(seed), 6)
    return {
        "fields": normal_values(key_list[0], (NLAT, NLON, C), 1.0, 6.0, ((0, 8), (1, 16))),
        "spectral_gain": normal_values(key_list[1], (L, 2, C), 1.0, 6.0, (), jnp.float32),
        "mix_weight": normal_values(key_list[2], (2, C, C), (2 * C) ** -0.5, 0.25),
        "column_list": jax.random.permutation(key_list[3], M).astype(jnp.int32),
        "column_counts": ragged(key_list[4], OWNERS, M, CAP, 1).astype(jnp.int32),
    }


def latitudes(total_rows, first_row, band_rows):
    position = (first_row + jnp.arange(band_rows, dtype=jnp.int32)).astype(jnp.float32)
    colatitude = math.pi * (position + 0.5) / total_rows
    return (jnp.cos(colatitude), jnp.sin(colatitude), math.pi / total_rows * jnp.sin(colatitude))

def fourier_table(orders, live_mask, lon_total):
    longitude = jnp.arange(lon_total, dtype=jnp.int32)
    wrapped = longitude[:, None] * orders[None, :] % lon_total
    angles = wrapped.astype(jnp.float32) * (2.0 * math.pi / lon_total)
    stacked = jnp.stack([jnp.cos(angles), -jnp.sin(angles)], axis=2)
    return (stacked * live_mask[None, :, None]).astype(jnp.bfloat16)

def legendre(orders, cosines, sines, degrees):
    order_col = orders[:, None]
    half_gamma = 0.5 * math.log(math.pi) - math.log(2.0)
    log_start = -0.5 * math.log(2.0) + 0.5 * (lax.lgamma(order_col + 1.5) - half_gamma - lax.lgamma(order_col + 1.0)) + order_col * jnp.log(sines)[None, :]
    zeros_now = jnp.zeros(log_start.shape, jnp.float32)
    ones_now = jnp.ones(log_start.shape, jnp.float32)

    def advance(carried, degree):
        previous, current, log_scale = carried
        level = degree.astype(jnp.float32)
        upper = jnp.sqrt(jnp.maximum(4.0 * level * level - 1.0, 0.0) / jnp.maximum(level * level - order_col * order_col, 1.0))
        lower = jnp.sqrt(jnp.maximum((level - 1.0) ** 2 - order_col * order_col, 0.0) / jnp.maximum(4.0 * (level - 1.0) ** 2 - 1.0, 1.0))
        advanced = upper * (cosines[None, :] * current - lower * previous)
        largest = jnp.maximum(jnp.abs(advanced), jnp.abs(current))
        moving = level > order_col
        safe_largest = jnp.where(moving, largest, 1.0)
        previous_new = jnp.where(moving, current / safe_largest, previous)
        current_new = jnp.where(moving, advanced / safe_largest, current)
        scale_new = jnp.where(moving, log_scale + jnp.log(safe_largest), log_scale)
        values_now = jnp.where(level < order_col, 0.0, current_new * jnp.exp(scale_new))
        return ((previous_new, current_new, scale_new), values_now)
    initial = (zeros_now, ones_now, log_start)
    _, stacked = lax.scan(advance, initial, jnp.arange(degrees, dtype=jnp.int32))
    return stacked

def apply_gain(spectra, spectral_gain):
    channels = spectral_gain.shape[2]
    real_part = spectra[..., :channels]
    imag_part = spectra[..., channels:]
    gain_real = spectral_gain[:, 0, :]
    gain_imag = spectral_gain[:, 1, :]
    return jnp.concatenate([gain_real * real_part - gain_imag * imag_part, gain_real * imag_part + gain_imag * real_part], axis=-1)

def complex_block(mix_weight):
    top_half = jnp.concatenate([mix_weight[0], mix_weight[1]], axis=1)
    bottom_half = jnp.concatenate([-mix_weight[1], mix_weight[0]], axis=1)
    return jnp.concatenate([top_half, bottom_half], axis=0)

def reference(fields, spectral_gain, mix_weight, column_list, column_counts):
    cosines, sines, weights = latitudes(NLAT, 0, NLAT)
    orders = jnp.arange(M, dtype=jnp.int32)
    fourier = fourier_table(orders, jnp.ones((M,), jnp.float32), NLON).astype(jnp.float32).reshape(NLON, 2 * M)
    band_rows = NLAT // N_LAT
    field_blocks = fields.reshape(N_LAT, band_rows, NLON, C)
    weight_blocks = weights.reshape(N_LAT, band_rows)

    def forward(pair):
        band, band_weights = pair
        summed = jnp.einsum('ajc,jq->aqc', band.astype(jnp.float32), fourier, precision=lax.Precision.HIGHEST)
        return (summed * band_weights[:, None, None]).astype(jnp.bfloat16)
    spectral_in = lax.map(forward, (field_blocks, weight_blocks)).reshape(NLAT, M, 2, C)
    run_ends = jnp.cumsum(column_counts)
    starts = run_ends - column_counts
    offsets = jnp.arange(CAP, dtype=jnp.int32)
    positions = jnp.minimum(starts[:, None] + offsets[None, :], M - 1)
    live_mask = (offsets[None, :] < column_counts[:, None]).astype(jnp.float32)
    slot_orders = column_list[positions]
    mixing = complex_block(mix_weight)

    def per_owner(owner_item):
        own_orders, own_live = owner_item
        columns = spectral_in[:, own_orders].astype(jnp.float32) * own_live[None, :, None, None]
        columns = columns.reshape(NLAT, CAP, 2 * C)
        rounded = lax.optimization_barrier(legendre(own_orders.astype(jnp.float32), cosines, sines, L).astype(jnp.bfloat16))
        associated = rounded.astype(jnp.float32)
        spectra = jnp.einsum('lsk,ksq->slq', associated, columns, precision=lax.Precision.HIGHEST)
        scaled = apply_gain(spectra, spectral_gain).astype(jnp.bfloat16)
        mixed_spec = jnp.dot(scaled.reshape(CAP * L, 2 * C), mixing, preferred_element_type=jnp.float32).astype(jnp.bfloat16).reshape(CAP, L, 2 * C)
        returned = jnp.einsum('lsk,slq->ksq', associated, mixed_spec.astype(jnp.float32), precision=lax.Precision.HIGHEST).astype(jnp.bfloat16)
        return (mixed_spec.reshape(CAP, L, 2, C), returned)
    spectrum, returned = lax.map(per_owner, (slot_orders, live_mask))
    flat_returned = returned.transpose(1, 0, 2, 3).reshape(NLAT, OWNERS * CAP, 2, C)
    gathered = jnp.zeros((NLAT, M, 2, C), jnp.bfloat16).at[:, slot_orders.reshape(-1)].add(flat_returned)
    factor = jnp.where(orders == 0, 1.0, 2.0).astype(jnp.bfloat16)
    gathered = (gathered * factor[None, :, None, None]).reshape(N_LAT, band_rows, 2 * M, C)

    def inverse(pair):
        band_spec, band = pair
        filtered = (jnp.einsum('aqc,jq->ajc', band_spec.astype(jnp.float32), fourier, precision=lax.Precision.HIGHEST) / float(NLON)).astype(jnp.bfloat16)
        return (band.astype(jnp.float32) + jax.nn.gelu(filtered.astype(jnp.float32), approximate=False)).astype(jnp.bfloat16)
    blended = lax.map(inverse, (gathered, field_blocks)).reshape(NLAT, NLON, C)
    return (blended, spectrum)
```

```python
import functools
import math

import jax
import jax.numpy as jnp
from jax import lax
from jax.experimental import pallas as pl
from jax.experimental.pallas import tpu as pltpu
from jax.sharding import PartitionSpec as P

QUARTERS = 4
UNIT = 8
UNITS = 3
PAIRS = UNIT // 2
LON_PAD = 96
HALF = 64
LANES = 128
SLOTS = 7
LEVELS = 768
ROWS = 768
ROW_CHUNKS = ((0, 2), (2, 3))
SLOT_CHUNKS = ((0, 4), (4, 7))
VMEM = 56 * 1024 * 1024
LEVEL_BLOCK = 128
RESCALE = 8


def call(kernel, name, flops, moved, **kwargs):
    return pl.pallas_call(
        kernel,
        name=name,
        compiler_params=pltpu.CompilerParams(vmem_limit_bytes=VMEM),
        cost_estimate=pl.CostEstimate(flops=flops, bytes_accessed=moved, transcendentals=0),
        **kwargs,
    )


def low_half():
    return lax.broadcasted_iota(jnp.int32, (1, LANES), 1) < HALF


def swap(value):
    return pltpu.roll(value, HALF, value.ndim - 1)


def join_low(first, second):
    return jnp.where(low_half(), first, swap(second))


def join_high(first, second):
    return jnp.where(low_half(), swap(first), second)


def pack_kernel(unit_first, band_rows, fields_ref, out_ref):
    lon_cols = fields_ref.shape[1]
    base = (pl.program_id(0) * UNITS + unit_first + pl.program_id(1)) * UNIT
    out_ref[...] = jnp.zeros_like(out_ref)
    for pair in range(PAIRS):
        first = fields_ref[2 * pair].astype(jnp.float32)
        second = fields_ref[2 * pair + 1].astype(jnp.float32)
        first = jnp.where(base + 2 * pair < band_rows, first, 0.0)
        second = jnp.where(base + 2 * pair + 1 < band_rows, second, 0.0)
        for tile in range(2):
            lanes = slice(tile * LANES, (tile + 1) * LANES)
            one, two = first[:, lanes], second[:, lanes]
            out_ref[0, 2 * tile, pair, :lon_cols] = join_low(one, two).astype(jnp.bfloat16)
            out_ref[0, 2 * tile + 1, pair, :lon_cols] = join_high(one, two).astype(jnp.bfloat16)


def pack(fields, chunk):
    band_rows, lon_cols, channels = fields.shape
    first, last = chunk
    count = last - first
    out = call(
        functools.partial(pack_kernel, first, band_rows),
        "pack",
        0,
        2 * 2 * count * UNIT * QUARTERS * LON_PAD * channels,
        grid=(QUARTERS, count),
        in_specs=[
            pl.BlockSpec((UNIT, lon_cols, channels), lambda q, u: (q * UNITS + first + u, 0, 0))
        ],
        out_specs=pl.BlockSpec(
            (1, QUARTERS, PAIRS, LON_PAD, LANES), lambda q, u: (q, 0, u, 0, 0)
        ),
        out_shape=jax.ShapeDtypeStruct(
            (QUARTERS, QUARTERS, count * PAIRS, LON_PAD, LANES), jnp.bfloat16
        ),
    )(fields)
    return out.reshape(QUARTERS * QUARTERS, count * PAIRS, LON_PAD, LANES)


def forward_kernel(chunk_count, has_alias, *refs):
    arrived_ref, table_ref, weight_ref = refs[:3]
    refs = refs[3 + (chunk_count if has_alias else 0) :]
    out_refs, matrix, turned = refs[:chunk_count], refs[chunk_count], refs[chunk_count + 1]
    sources = arrived_ref.shape[0]
    for pair in range(PAIRS):
        matrix[:, pair * LANES : (pair + 1) * LANES] = arrived_ref[:, pair].reshape(
            sources * LON_PAD, LANES
        )
    weights = weight_ref[0]
    owners = table_ref.shape[2]

    def one_slot(slot, out_ref, place):
        table = table_ref[slot].reshape(2 * owners, sources * LON_PAD)
        summed = jnp.dot(table, matrix[...], preferred_element_type=jnp.float32) * weights
        for pair in range(PAIRS):
            real = summed[:owners, pair * LANES : (pair + 1) * LANES]
            imag = summed[owners:, pair * LANES : (pair + 1) * LANES]
            turned[pl.ds(2 * pair, owners, stride=UNIT), :] = join_low(real, imag)
            turned[pl.ds(2 * pair + 1, owners, stride=UNIT), :] = join_high(real, imag)
        out_ref[:, place, 0] = turned[...].reshape(owners, UNIT, LANES).astype(jnp.bfloat16)

    for out_ref, (start, stop) in zip(out_refs, SLOT_CHUNKS):

        def step(place, carry, out_ref=out_ref, start=start):
            one_slot(start + place, out_ref, place)
            return carry

        lax.fori_loop(0, stop - start, step, 0)


def forward(arrived, table, weights, chunk, buffers):
    first, last = chunk
    count = last - first
    sources = arrived.shape[0]
    owners = table.shape[2]
    shapes = [
        jax.ShapeDtypeStruct((owners, stop - start, UNITS, UNIT, LANES), jnp.bfloat16)
        for start, stop in SLOT_CHUNKS
    ]
    has_alias = buffers is not None
    operands = [arrived, table, weights] + (list(buffers) if has_alias else [])
    return call(
        functools.partial(forward_kernel, len(shapes), has_alias),
        "forward",
        2 * count * table.size * PAIRS * LANES,
        2 * (arrived.size + table.size),
        grid=(count,),
        in_specs=[
            pl.BlockSpec((sources, PAIRS, LON_PAD, LANES), lambda u: (0, u, 0, 0)),
            pl.BlockSpec(table.shape, lambda u: (0, 0, 0, 0)),
            pl.BlockSpec((1, 1, PAIRS * LANES), lambda u: (first + u, 0, 0)),
        ]
        + ([pl.BlockSpec(memory_space=pl.ANY)] * len(shapes) if has_alias else []),
        out_specs=[
            pl.BlockSpec((owners, s.shape[1], 1, UNIT, LANES), lambda u: (0, 0, first + u, 0, 0))
            for s in shapes
        ],
        out_shape=shapes,
        scratch_shapes=[
            pltpu.VMEM((sources * LON_PAD, PAIRS * LANES), jnp.bfloat16),
            pltpu.VMEM((owners * UNIT, LANES), jnp.float32),
        ],
        input_output_aliases={3 + i: i for i in range(len(shapes))} if has_alias else {},
    )(*operands)


def middle_kernel(has_alias, *refs):
    arrived_ref, table_ref, turned_ref, gain_ref, cross_ref, mixing_ref = refs[:6]
    spectrum_ref, out_ref = refs[7:] if has_alias else refs[6:]
    degrees = spectrum_ref.shape[1]
    arrived = arrived_ref[:, 0].astype(jnp.float32)
    groups = arrived.shape[0] // QUARTERS
    arrived = arrived.reshape(groups, QUARTERS, UNITS * UNIT, LANES)
    columns = jnp.concatenate(
        [
            arrived[:, quarter].reshape(ROWS, LANES).astype(jnp.bfloat16)
            for quarter in range(QUARTERS)
        ],
        axis=1,
    )
    spectra = jnp.dot(table_ref[0], columns, preferred_element_type=jnp.float32)
    parts = []
    for quarter in range(QUARTERS):
        lanes = slice(quarter * LANES, (quarter + 1) * LANES)
        piece = spectra[:, lanes]
        parts.append(
            (gain_ref[:, lanes] * piece + cross_ref[:, lanes] * swap(piece)).astype(jnp.bfloat16)
        )
    scaled = jnp.concatenate(parts, axis=1)
    mixed = jnp.dot(scaled, mixing_ref[...], preferred_element_type=jnp.float32)
    pieces = [mixed[:, q * LANES : (q + 1) * LANES] for q in range(QUARTERS)]
    for tile in range(2):
        one, two = pieces[2 * tile][:degrees], pieces[2 * tile + 1][:degrees]
        lanes = slice(tile * LANES, (tile + 1) * LANES)
        spectrum_ref[0, :, lanes] = join_low(one, two).astype(jnp.bfloat16)
        lanes = slice((2 + tile) * LANES, (3 + tile) * LANES)
        spectrum_ref[0, :, lanes] = join_high(one, two).astype(jnp.bfloat16)
    returned = jnp.dot(
        turned_ref[0], mixed.astype(jnp.bfloat16), preferred_element_type=jnp.float32
    )
    for quarter in range(QUARTERS):
        piece = returned[:, quarter * LANES : (quarter + 1) * LANES]
        out_ref[:, quarter, 0] = piece.reshape(groups, UNITS, UNIT, LANES).astype(jnp.bfloat16)


def middle(arrived, table, turned, gain, cross, mixing, slots, degrees, spectrum):
    start, stop = slots
    owners = arrived.shape[0]
    groups = owners // QUARTERS
    width = mixing.shape[0]
    has_alias = spectrum is not None
    operands = [arrived, table, turned, gain, cross, mixing] + ([spectrum] if has_alias else [])
    spectrum, out = call(
        functools.partial(middle_kernel, has_alias),
        "middle",
        2 * (stop - start) * LEVELS * width * (2 * ROWS + width),
        (stop - start) * (4 * LEVELS * ROWS + 6 * LEVELS * width),
        grid=(stop - start,),
        in_specs=[
            pl.BlockSpec((owners, 1, UNITS, UNIT, LANES), lambda s: (0, s, 0, 0, 0)),
            pl.BlockSpec((1, LEVELS, ROWS), lambda s: (start + s, 0, 0)),
            pl.BlockSpec((1, ROWS, LEVELS), lambda s: (start + s, 0, 0)),
            pl.BlockSpec(gain.shape, lambda s: (0, 0)),
            pl.BlockSpec(cross.shape, lambda s: (0, 0)),
            pl.BlockSpec(mixing.shape, lambda s: (0, 0)),
        ]
        + ([pl.BlockSpec(memory_space=pl.ANY)] if has_alias else []),
        out_specs=[
            pl.BlockSpec((1, degrees, width), lambda s: (start + s, 0, 0)),
            pl.BlockSpec((groups, QUARTERS, 1, UNITS, UNIT, LANES), lambda s: (0, 0, s, 0, 0, 0)),
        ],
        out_shape=[
            jax.ShapeDtypeStruct((SLOTS, degrees, width), jnp.bfloat16),
            jax.ShapeDtypeStruct(
                (groups, QUARTERS, stop - start, UNITS, UNIT, LANES), jnp.bfloat16
            ),
        ],
        input_output_aliases={6: 0} if has_alias else {},
    )(*operands)
    return spectrum, out.reshape(owners, stop - start, UNITS, UNIT, LANES)


def inverse_kernel(scale, chunk_count, *refs):
    arrived_refs, table_ref, out_ref = refs[:chunk_count], refs[chunk_count], refs[chunk_count + 1]
    wide, matrix = refs[chunk_count + 2], refs[chunk_count + 3]
    owners = arrived_refs[0].shape[0]
    for arrived_ref, (start, stop) in zip(arrived_refs, SLOT_CHUNKS):

        def one_slot(place, carry, arrived_ref=arrived_ref, start=start):
            wide[...] = arrived_ref[:, place, 0].astype(jnp.float32).reshape(owners * UNIT, LANES)
            row = pl.multiple_of((start + place) * 2 * owners, 2 * owners)
            for pair in range(PAIRS):
                one = wide[pl.ds(2 * pair, owners, stride=UNIT), :]
                two = wide[pl.ds(2 * pair + 1, owners, stride=UNIT), :]
                lanes = slice(pair * LANES, (pair + 1) * LANES)
                matrix[pl.ds(row, owners), lanes] = join_low(one, two).astype(jnp.bfloat16)
                matrix[pl.ds(row + owners, owners), lanes] = join_high(one, two).astype(
                    jnp.bfloat16
                )
            return carry

        lax.fori_loop(0, stop - start, one_slot, 0)
    blocks = 4
    rows = blocks * LON_PAD

    def some_columns(step, carry):
        row = pl.multiple_of(step * rows, rows)
        summed = jnp.dot(
            table_ref[pl.ds(row, rows), :], matrix[...], preferred_element_type=jnp.float32
        )
        summed = (summed * scale).astype(jnp.bfloat16)
        for pair in range(PAIRS):
            out_ref[pl.ds(step * blocks, blocks), pair] = summed[
                :, pair * LANES : (pair + 1) * LANES
            ].reshape(blocks, LON_PAD, LANES)
        return carry

    lax.fori_loop(0, table_ref.shape[0] // rows, some_columns, 0)


def inverse(arrived, table, chunk, lon_total):
    first, last = chunk
    count = last - first
    owners = arrived[0].shape[0]
    targets = table.shape[0] // LON_PAD
    return call(
        functools.partial(inverse_kernel, 1.0 / lon_total, len(arrived)),
        "inverse",
        2 * count * table.size * PAIRS * LANES,
        2 * 2 * table.size,
        grid=(count,),
        in_specs=[
            pl.BlockSpec((owners, a.shape[1], 1, UNIT, LANES), lambda u: (0, 0, first + u, 0, 0))
            for a in arrived
        ]
        + [pl.BlockSpec(table.shape, lambda u: (0, 0))],
        out_specs=pl.BlockSpec((targets, PAIRS, LON_PAD, LANES), lambda u: (0, u, 0, 0)),
        out_shape=jax.ShapeDtypeStruct((targets, count * PAIRS, LON_PAD, LANES), jnp.bfloat16),
        scratch_shapes=[
            pltpu.VMEM((owners * UNIT, LANES), jnp.float32),
            pltpu.VMEM((table.shape[1], PAIRS * LANES), jnp.bfloat16),
        ],
    )(*arrived, table)


def blend_kernel(has_alias, *refs):
    arrived_ref, fields_ref = refs[:2]
    out_ref = refs[-1]
    lon_cols = fields_ref.shape[1]

    def gelu(value):
        return 0.5 * value * (1.0 + lax.erf(value * math.sqrt(0.5)))

    for pair in range(PAIRS):
        for tile in range(2):
            lanes = slice(tile * LANES, (tile + 1) * LANES)
            one = gelu(arrived_ref[0, 2 * tile, pair, :lon_cols].astype(jnp.float32))
            two = gelu(arrived_ref[0, 2 * tile + 1, pair, :lon_cols].astype(jnp.float32))
            for row, value in ((2 * pair, join_low(one, two)), (2 * pair + 1, join_high(one, two))):
                held = fields_ref[row, :, lanes].astype(jnp.float32)
                out_ref[row, :, lanes] = (held + value).astype(jnp.bfloat16)


def blend(arrived, fields, chunk, buffer):
    first, last = chunk
    count = last - first
    band_rows, lon_cols, channels = fields.shape
    has_alias = buffer is not None
    arrived = arrived.reshape(QUARTERS, QUARTERS, count * PAIRS, LON_PAD, LANES)
    held = pl.BlockSpec((UNIT, lon_cols, channels), lambda q, u: (q * UNITS + first + u, 0, 0))
    return call(
        functools.partial(blend_kernel, has_alias),
        "blend",
        60 * count * UNIT * QUARTERS * lon_cols * channels,
        6 * count * UNIT * QUARTERS * lon_cols * channels,
        grid=(QUARTERS, count),
        in_specs=[
            pl.BlockSpec((1, QUARTERS, PAIRS, LON_PAD, LANES), lambda q, u: (q, 0, u, 0, 0)),
            held,
        ]
        + ([pl.BlockSpec(memory_space=pl.ANY)] if has_alias else []),
        out_specs=held,
        out_shape=jax.ShapeDtypeStruct(fields.shape, fields.dtype),
        input_output_aliases={2: 0} if has_alias else {},
    )(arrived, fields, *([buffer] if has_alias else []))


def legendre_kernel(degrees, order_ref, start_ref, lat_ref, out_ref, state, rows):
    tiles = ROWS // LANES
    order = order_ref[...]

    @pl.when(pl.program_id(0) == 0)
    def _():
        for tile in range(tiles):
            lanes = slice(tile * LANES, (tile + 1) * LANES)
            state[0, :, lanes] = jnp.zeros_like(order)
            state[1, :, lanes] = jnp.ones_like(order)
            state[2, :, lanes] = start_ref[...] + order * jnp.log(lat_ref[1:2, lanes])

    def pieces(index):
        return tuple(state[index, :, t * LANES : (t + 1) * LANES] for t in range(tiles))

    cosines = tuple(lat_ref[0:1, t * LANES : (t + 1) * LANES] for t in range(tiles))
    first = pl.program_id(0) * LEVEL_BLOCK

    def group(index, carry):
        previous, current, log_scale = [list(part) for part in carry]
        halves = []
        for tile in range(tiles):
            largest = jnp.maximum(jnp.abs(previous[tile]), jnp.abs(current[tile]))
            shrink = 1.0 / largest
            previous[tile] = previous[tile] * shrink
            current[tile] = current[tile] * shrink
            log_scale[tile] = log_scale[tile] + jnp.log(largest)
            halves.append(jnp.exp(0.5 * log_scale[tile]))
        for inner in range(RESCALE):
            level = (first + index * RESCALE + inner).astype(jnp.float32)
            square = (level - 1.0) * (level - 1.0)
            upper = jnp.sqrt(
                jnp.maximum(4.0 * level * level - 1.0, 0.0)
                / jnp.maximum(level * level - order * order, 1.0)
            )
            lower = jnp.sqrt(
                jnp.maximum(square - order * order, 0.0) / jnp.maximum(4.0 * square - 1.0, 1.0)
            )
            moving = level > order
            shown = jnp.logical_and(level >= order, level < degrees)
            row = pl.multiple_of((index * RESCALE + inner) * 8, 8)
            for tile in range(tiles):
                advanced = upper * (cosines[tile] * current[tile] - lower * previous[tile])
                previous[tile] = jnp.where(moving, current[tile], previous[tile])
                current[tile] = jnp.where(moving, advanced, current[tile])
                value = (current[tile] * halves[tile]) * halves[tile]
                rows[tile, pl.ds(row, 8), :] = jnp.where(shown, value, 0.0)
        return tuple(previous), tuple(current), tuple(log_scale)

    done = lax.fori_loop(
        0, LEVEL_BLOCK // RESCALE, group, (pieces(0), pieces(1), pieces(2))
    )
    for index in range(3):
        for tile in range(tiles):
            state[index, :, tile * LANES : (tile + 1) * LANES] = done[index][tile]
    for slot in range(SLOTS):
        for tile in range(tiles):
            out_ref[slot, :, tile * LANES : (tile + 1) * LANES] = rows[
                tile, pl.ds(slot, LEVEL_BLOCK, stride=8), :
            ].astype(jnp.bfloat16)


def legendre(orders, colatitude, degrees):
    order_col = orders.astype(jnp.float32)
    half_gamma = 0.5 * math.log(math.pi) - math.log(2.0)
    log_start = -0.5 * math.log(2.0) + 0.5 * (
        lax.lgamma(order_col + 1.5) - half_gamma - lax.lgamma(order_col + 1.0)
    )
    widen = lambda a: jnp.broadcast_to(jnp.pad(a, (0, 8 - SLOTS))[:, None], (8, LANES))
    lat = jnp.stack([jnp.cos(colatitude), jnp.sin(colatitude)])
    return call(
        functools.partial(legendre_kernel, degrees),
        "legendre",
        30 * LEVELS * 8 * ROWS,
        2 * SLOTS * LEVELS * ROWS,
        grid=(LEVELS // LEVEL_BLOCK,),
        in_specs=[
            pl.BlockSpec((8, LANES), lambda i: (0, 0)),
            pl.BlockSpec((8, LANES), lambda i: (0, 0)),
            pl.BlockSpec((2, ROWS), lambda i: (0, 0)),
        ],
        out_specs=pl.BlockSpec((SLOTS, LEVEL_BLOCK, ROWS), lambda i: (0, i, 0)),
        out_shape=jax.ShapeDtypeStruct((SLOTS, LEVELS, ROWS), jnp.bfloat16),
        scratch_shapes=[
            pltpu.VMEM((3, 8, ROWS), jnp.float32),
            pltpu.VMEM((ROWS // LANES, LEVEL_BLOCK * 8, LANES), jnp.float32),
        ],
    )(widen(order_col), widen(log_start), lat)


def fourier_tables(orders, live, lon_devices, lon_cols):
    lon_total = lon_devices * lon_cols
    place = jnp.arange(lon_devices * LON_PAD, dtype=jnp.int32)
    block, inside = place // LON_PAD, place % LON_PAD
    longitude = (block * lon_cols + inside).astype(jnp.float32)
    product = orders.astype(jnp.float32)[:, :, None] * longitude
    wrapped = product - lon_total * jnp.floor(product * (1.0 / lon_total))
    wrapped = jnp.where(wrapped < 0, wrapped + lon_total, wrapped)
    wrapped = jnp.where(wrapped >= lon_total, wrapped - lon_total, wrapped)
    angles = wrapped * (2.0 * math.pi / lon_total)
    mask = live[:, :, None] * (inside < lon_cols).astype(jnp.float32)
    return jnp.stack([jnp.cos(angles) * mask, -jnp.sin(angles) * mask], axis=1).astype(jnp.bfloat16)


def regroup(array, axis):
    shape = array.shape
    split = shape[:axis] + (2, QUARTERS, HALF) + shape[axis + 1 :]
    return jnp.swapaxes(array.reshape(split), axis, axis + 1).reshape(shape)


def complex_block(mix_weight):
    top_half = jnp.concatenate([mix_weight[0], mix_weight[1]], axis=1)
    bottom_half = jnp.concatenate([-mix_weight[1], mix_weight[0]], axis=1)
    return jnp.concatenate([top_half, bottom_half], axis=0)


def exchange(array, axes):
    return lax.all_to_all(array, axes, split_axis=0, concat_axis=0, tiled=True)


def shards(fields, spectral_gain, mix_weight, column_list, column_counts):
    band_rows, lon_cols, channels = fields.shape
    lat_devices = lax.axis_size("lat")
    lon_devices = lax.axis_size("lon")
    owners = lat_devices * lon_devices
    lat_total = band_rows * lat_devices
    lon_total = lon_cols * lon_devices
    degrees = spectral_gain.shape[0]
    mode_count = column_list.shape[0]

    gathered = [exchange(pack(fields, chunk), "lon") for chunk in ROW_CHUNKS]

    run_ends = jnp.cumsum(column_counts)
    starts = run_ends - column_counts
    offsets = jnp.arange(SLOTS, dtype=jnp.int32)
    positions = jnp.minimum(starts[None, :] + offsets[:, None], mode_count - 1)
    live = (offsets[:, None] < column_counts[None, :]).astype(jnp.float32)
    matches = positions[:, :, None] == jnp.arange(mode_count, dtype=jnp.int32)
    slot_orders = jnp.sum(jnp.where(matches, column_list, 0), axis=2)
    table = fourier_tables(slot_orders, live, lon_devices, lon_cols)
    factor = jnp.where(slot_orders == 0, 1.0, 2.0).astype(jnp.bfloat16)
    back_table = (table * factor[:, None, :, None]).reshape(
        SLOTS * 2 * owners, lon_devices * LON_PAD
    ).T

    owner_index = lax.axis_index(("lat", "lon"))
    own_orders = lax.dynamic_slice_in_dim(slot_orders, owner_index, 1, axis=1)[:, 0]
    padded = jnp.arange(ROWS, dtype=jnp.int32)
    band, inside = padded // (ROWS // lat_devices), padded % (ROWS // lat_devices)
    row = (band * band_rows + jnp.minimum(inside, band_rows - 1)).astype(jnp.float32)
    associated = legendre(own_orders, math.pi * (row + 0.5) / lat_total, degrees)
    turned = jnp.swapaxes(associated, 1, 2)

    group = lax.axis_index("lon") // QUARTERS
    mine = jnp.arange(UNITS * UNIT, dtype=jnp.int32) + group * (UNITS * UNIT)
    mine = (lax.axis_index("lat") * band_rows + mine).astype(jnp.float32)
    weights = math.pi / lat_total * jnp.sin(math.pi * (mine + 0.5) / lat_total)
    weights = jnp.repeat(weights.reshape(UNITS, 1, UNIT), HALF, axis=2)

    real, imag = spectral_gain[:, 0], spectral_gain[:, 1]
    fill = ((0, LEVELS - degrees), (0, 0))
    gain = jnp.pad(regroup(jnp.concatenate([real, real], axis=1), 1), fill)
    cross = jnp.pad(regroup(jnp.concatenate([-imag, imag], axis=1), 1), fill)
    mixing = regroup(regroup(complex_block(mix_weight), 0), 1)

    sends = None
    for chunk, arrived in zip(ROW_CHUNKS, gathered):
        sends = forward(arrived, table, weights, chunk, sends)
    arrived = [exchange(send, ("lat", "lon")) for send in sends]
    spectrum, landed = None, []
    for slots, part in zip(SLOT_CHUNKS, arrived):
        spectrum, send = middle(
            part, associated, turned, gain, cross, mixing, slots, degrees, spectrum
        )
        landed.append(exchange(send, ("lat", "lon")))
    blended = None
    for chunk in ROW_CHUNKS:
        home = exchange(inverse(landed, back_table, chunk, lon_total), "lon")
        blended = blend(home, fields, chunk, blended)
    return blended, spectrum.reshape(1, SLOTS, degrees, 2, channels)


def solution(mesh):
    placed = (P("lat", "lon", None), P(), P(), P(), P())
    return jax.shard_map(
        shards,
        mesh=mesh,
        in_specs=placed,
        out_specs=(P("lat", "lon", None), P(("lat", "lon"), None, None, None, None)),
        check_vma=False,
    )
```

```python
import functools
import math

import jax
import jax.numpy as jnp
from jax import lax
from jax.experimental import pallas as pl
from jax.experimental.pallas import tpu as pltpu
from jax.sharding import PartitionSpec as P

QUARTERS = 4
UNIT = 8
UNITS = 3
PAIRS = UNIT // 2
LON_PAD = 96
GROUP = 16
HALF = 64
LANES = 128
SLOTS = 7
LEVELS = 768
ROWS = 768
HOME_CHUNKS = ((0, 3),)
SLOT_CHUNKS = ((0, 3), (3, 7))
VMEM = 60
SEND_VMEM = 54
LESS_VMEM = 28
LEVEL_BLOCK = 128
RESCALE = 8


def call(
    kernel, name, flops, moved, operands, in_specs, after=(), aliases=(), vmem=VMEM, **kwargs
):
    known = len(operands)
    extra = list(after) + list(aliases)

    def body(*refs):
        kernel(*refs[:known], *refs[known + len(extra) :])

    return pl.pallas_call(
        body,
        name=name,
        compiler_params=pltpu.CompilerParams(vmem_limit_bytes=vmem * 1024 * 1024),
        cost_estimate=pl.CostEstimate(flops=flops, bytes_accessed=moved, transcendentals=0),
        in_specs=list(in_specs) + [pl.BlockSpec(memory_space=pl.ANY)] * len(extra),
        input_output_aliases={known + len(after) + i: i for i in range(len(aliases))},
        **kwargs,
    )(*operands, *extra)


def low_half():
    return lax.broadcasted_iota(jnp.int32, (1, LANES), 1) < HALF


def swap(value):
    return pltpu.roll(value, HALF, value.ndim - 1)


def join_low(first, second):
    return jnp.where(low_half(), first, swap(second))


def join_high(first, second):
    return jnp.where(low_half(), swap(first), second)


def exchange_rows(outer, inner):
    row = lax.broadcasted_iota(jnp.int32, (outer * inner, outer * inner), 0)
    column = lax.broadcasted_iota(jnp.int32, (outer * inner, outer * inner), 1)
    return (column == (row % inner) * outer + row // inner).astype(jnp.bfloat16)


def pack_kernel(band_rows, fields_ref, out_ref):
    rows, lon_cols = fields_ref.shape[:2]
    base = pl.program_id(0) * rows
    out_ref[0, :, :, lon_cols:, :] = jnp.zeros(
        (QUARTERS, rows // 2, LON_PAD - lon_cols, LANES), jnp.bfloat16
    )

    def one_pair(pair, carry):
        first = fields_ref[2 * pair].astype(jnp.float32)
        second = fields_ref[2 * pair + 1].astype(jnp.float32)
        first = jnp.where(base + 2 * pair < band_rows, first, 0.0)
        second = jnp.where(base + 2 * pair + 1 < band_rows, second, 0.0)
        for tile in range(2):
            lanes = slice(tile * LANES, (tile + 1) * LANES)
            one, two = first[:, lanes], second[:, lanes]
            out_ref[0, 2 * tile, pair, :lon_cols] = join_low(one, two).astype(jnp.bfloat16)
            out_ref[0, 2 * tile + 1, pair, :lon_cols] = join_high(one, two).astype(jnp.bfloat16)
        return carry

    lax.fori_loop(0, rows // 2, one_pair, 0)


def pack(fields, after):
    band_rows, lon_cols, channels = fields.shape
    rows = UNITS * UNIT
    out = call(
        functools.partial(pack_kernel, band_rows),
        "pack",
        0,
        4 * rows * QUARTERS * LON_PAD * channels,
        operands=[fields],
        after=after,
        vmem=SEND_VMEM,
        grid=(QUARTERS,),
        in_specs=[pl.BlockSpec((rows, lon_cols, channels), lambda q: (q, 0, 0))],
        out_specs=pl.BlockSpec(
            (1, QUARTERS, rows // 2, LON_PAD, LANES), lambda q: (q, 0, 0, 0, 0)
        ),
        out_shape=jax.ShapeDtypeStruct(
            (QUARTERS, QUARTERS, rows // 2, LON_PAD, LANES), jnp.bfloat16
        ),
    )
    return out.reshape(QUARTERS * QUARTERS, rows // 2, LON_PAD, LANES)


def forward_kernel(arrived_ref, table_ref, weight_ref, out_ref, matrix, summed):
    sources = arrived_ref.shape[0]
    slots, _, owners, longitudes = table_ref.shape
    for pair in range(PAIRS):
        matrix[:, pair * LANES : (pair + 1) * LANES] = arrived_ref[:, pair].reshape(
            sources * LON_PAD, LANES
        )
    table = table_ref[...].reshape(slots * 2 * owners, longitudes)
    summed[...] = jnp.dot(table, matrix[...], preferred_element_type=jnp.float32)
    turn = exchange_rows(GROUP, UNIT)
    weights = weight_ref[0]

    def one_slot(slot, carry):
        rows = []
        base = pl.multiple_of(slot * 2 * owners, 2 * owners)
        for pair in range(PAIRS):
            lanes = slice(pair * LANES, (pair + 1) * LANES)
            real = summed[pl.ds(base, owners), lanes] * weights[:, lanes]
            imag = summed[pl.ds(base + owners, owners), lanes] * weights[:, lanes]
            rows.append(join_low(real, imag).astype(jnp.bfloat16))
            rows.append(join_high(real, imag).astype(jnp.bfloat16))
        for first in range(0, owners, 2 * GROUP):
            both = jnp.concatenate(
                [
                    jnp.concatenate([row[start : start + GROUP] for row in rows], axis=0)
                    for start in (first, first + GROUP)
                ],
                axis=1,
            )
            both = jnp.dot(turn, both, preferred_element_type=jnp.float32)
            for half in range(2):
                piece = both[:, half * LANES : (half + 1) * LANES].reshape(GROUP, UNIT, LANES)
                start = first + half * GROUP
                out_ref[start : start + GROUP, slot, 0] = piece.astype(jnp.bfloat16)
        return carry

    lax.fori_loop(0, slots, one_slot, 0)


def forward(arrived, table, weights, slots, after=()):
    start, stop = slots
    sources = arrived.shape[0]
    owners, longitudes = table.shape[2:]
    work = UNITS * (stop - start)
    return call(
        forward_kernel,
        "forward",
        2 * work * 2 * owners * longitudes * PAIRS * LANES,
        2 * (arrived.size + (stop - start) * 2 * owners * longitudes),
        operands=[arrived, table, weights],
        after=after,
        vmem=SEND_VMEM,
        grid=(UNITS,),
        in_specs=[
            pl.BlockSpec((sources, PAIRS, LON_PAD, LANES), lambda u: (0, u, 0, 0)),
            pl.BlockSpec((stop - start, 2, owners, longitudes), lambda u: (0, 0, 0, 0)),
            pl.BlockSpec((1, 1, PAIRS * LANES), lambda u: (u, 0, 0)),
        ],
        out_specs=pl.BlockSpec(
            (owners, stop - start, 1, UNIT, LANES), lambda u: (0, 0, u, 0, 0)
        ),
        out_shape=jax.ShapeDtypeStruct((owners, stop - start, UNITS, UNIT, LANES), jnp.bfloat16),
        scratch_shapes=[
            pltpu.VMEM((sources * LON_PAD, PAIRS * LANES), jnp.bfloat16),
            pltpu.VMEM(((stop - start) * 2 * owners, PAIRS * LANES), jnp.float32),
        ],
    )


def middle_kernel(arrived_ref, table_ref, gain_ref, mixing_ref, spectrum_ref, out_ref):
    degrees, width = gain_ref.shape
    arrived = arrived_ref[:, 0].astype(jnp.float32)
    groups = arrived.shape[0] // QUARTERS
    arrived = arrived.reshape(groups, QUARTERS, UNITS * UNIT, LANES)
    columns = jnp.concatenate(
        [
            arrived[:, quarter].reshape(ROWS, LANES).astype(jnp.bfloat16)
            for quarter in range(QUARTERS)
        ],
        axis=1,
    )
    spectra = jnp.dot(table_ref[0, :degrees], columns, preferred_element_type=jnp.float32)
    parts = []
    for quarter in range(QUARTERS):
        tile = quarter // 2
        real = gain_ref[:, tile * LANES : (tile + 1) * LANES]
        imag = gain_ref[:, (2 + tile) * LANES : (3 + tile) * LANES]
        join = join_high if quarter % 2 else join_low
        piece = spectra[:, quarter * LANES : (quarter + 1) * LANES]
        piece = join(real, real) * piece + join(-imag, imag) * swap(piece)
        parts.append(piece.astype(jnp.bfloat16))
    scaled = jnp.concatenate(parts, axis=1)
    mixed = jnp.dot(scaled, mixing_ref[...], preferred_element_type=jnp.float32)
    pieces = [mixed[:, q * LANES : (q + 1) * LANES] for q in range(QUARTERS)]
    for tile in range(2):
        one, two = pieces[2 * tile], pieces[2 * tile + 1]
        lanes = slice(tile * LANES, (tile + 1) * LANES)
        spectrum_ref[0, :, lanes] = join_low(one, two).astype(jnp.bfloat16)
        lanes = slice((2 + tile) * LANES, (3 + tile) * LANES)
        spectrum_ref[0, :, lanes] = join_high(one, two).astype(jnp.bfloat16)
    filled = jnp.concatenate(
        [mixed.astype(jnp.bfloat16), jnp.zeros((LEVELS - degrees, width), jnp.bfloat16)], axis=0
    )
    returned = lax.dot_general(
        table_ref[0], filled, (((0,), (0,)), ((), ())), preferred_element_type=jnp.float32
    )
    for quarter in range(QUARTERS):
        piece = returned[:, quarter * LANES : (quarter + 1) * LANES]
        out_ref[:, quarter, 0] = piece.reshape(groups, UNITS, UNIT, LANES).astype(jnp.bfloat16)


def middle(arrived, table, gain, mixing, slots, after=()):
    start, stop = slots
    owners = arrived.shape[0]
    groups = owners // QUARTERS
    degrees, width = gain.shape
    spectrum, out = call(
        middle_kernel,
        "middle",
        2 * (stop - start) * LEVELS * width * (2 * ROWS + width),
        (stop - start) * (4 * LEVELS * ROWS + 6 * LEVELS * width),
        operands=[arrived, table, gain, mixing],
        after=after,
        grid=(stop - start,),
        in_specs=[
            pl.BlockSpec((owners, 1, UNITS, UNIT, LANES), lambda s: (0, s, 0, 0, 0)),
            pl.BlockSpec((1, LEVELS, ROWS), lambda s: (start + s, 0, 0)),
            pl.BlockSpec(gain.shape, lambda s: (0, 0)),
            pl.BlockSpec(mixing.shape, lambda s: (0, 0)),
        ],
        out_specs=[
            pl.BlockSpec((1, degrees, width), lambda s: (s, 0, 0)),
            pl.BlockSpec((groups, QUARTERS, 1, UNITS, UNIT, LANES), lambda s: (0, 0, s, 0, 0, 0)),
        ],
        out_shape=[
            jax.ShapeDtypeStruct((stop - start, degrees, width), jnp.bfloat16),
            jax.ShapeDtypeStruct(
                (groups, QUARTERS, stop - start, UNITS, UNIT, LANES), jnp.bfloat16
            ),
        ],
    )
    return spectrum, out.reshape(owners, stop - start, UNITS, UNIT, LANES)


def inverse_kernel(scale, has_partial, *refs):
    arrived_ref, table_ref = refs[:2]
    partial_ref = refs[2] if has_partial else None
    out_ref, matrix = refs[-2:]
    owners, slots = arrived_ref.shape[:2]

    def one_slot(slot, carry):
        row = pl.multiple_of(slot * 2 * owners, 2 * owners)
        turn = exchange_rows(UNIT, GROUP)
        wide = arrived_ref[:, slot, 0].astype(jnp.float32).reshape(owners * UNIT, LANES)
        wide = wide.astype(jnp.bfloat16)
        size = GROUP * UNIT
        groups = []
        for first in range(0, owners * UNIT, 2 * size):
            both = jnp.concatenate(
                [wide[first : first + size], wide[first + size : first + 2 * size]], axis=1
            )
            both = jnp.dot(turn, both, preferred_element_type=jnp.float32)
            groups += [both[:, :LANES], both[:, LANES:]]
        for pair in range(PAIRS):
            one, two = [
                jnp.concatenate([g[k * GROUP : (k + 1) * GROUP] for g in groups], axis=0)
                for k in (2 * pair, 2 * pair + 1)
            ]
            lanes = slice(pair * LANES, (pair + 1) * LANES)
            matrix[pl.ds(row, owners), lanes] = join_low(one, two).astype(jnp.bfloat16)
            matrix[pl.ds(row + owners, owners), lanes] = join_high(one, two).astype(
                jnp.bfloat16
            )
        return carry

    lax.fori_loop(0, slots, one_slot, 0)

    summed = jnp.dot(table_ref[...], matrix[...], preferred_element_type=jnp.float32)
    if not has_partial:
        out_ref[0] = summed
        return
    summed = ((summed + partial_ref[0]) * scale).astype(jnp.bfloat16)
    for pair in range(PAIRS):
        lanes = slice(pair * LANES, (pair + 1) * LANES)
        out_ref[:, pair] = summed[:, lanes].reshape(-1, LON_PAD, LANES)


def inverse(arrived, table, chunk, lon_total, partial=None, after=()):
    first, last = chunk
    count = last - first
    owners, slots = arrived.shape[:2]
    targets = table.shape[0] // LON_PAD
    has_partial = partial is not None
    summed = pl.BlockSpec((1, table.shape[0], PAIRS * LANES), lambda u: (u, 0, 0))
    if has_partial:
        spec = pl.BlockSpec((targets, PAIRS, LON_PAD, LANES), lambda u: (0, u, 0, 0))
        shape = jax.ShapeDtypeStruct((targets, count * PAIRS, LON_PAD, LANES), jnp.bfloat16)
    else:
        spec = summed
        shape = jax.ShapeDtypeStruct((count, table.shape[0], PAIRS * LANES), jnp.float32)
    return call(
        functools.partial(inverse_kernel, 1.0 / lon_total, has_partial),
        "inverse",
        2 * count * table.size * PAIRS * LANES,
        2 * 2 * table.size,
        operands=[arrived, table] + ([partial] if has_partial else []),
        after=after,
        vmem=SEND_VMEM if has_partial else VMEM,
        grid=(count,),
        in_specs=[
            pl.BlockSpec((owners, slots, 1, UNIT, LANES), lambda u: (0, 0, first + u, 0, 0)),
            pl.BlockSpec(table.shape, lambda u: (0, 0)),
        ]
        + ([summed] if has_partial else []),
        out_specs=spec,
        out_shape=shape,
        scratch_shapes=[pltpu.VMEM((table.shape[1], PAIRS * LANES), jnp.bfloat16)],
    )


def blend_kernel(arrived_ref, fields_ref, out_ref):
    lon_cols = fields_ref.shape[1]

    def gelu(value):
        return 0.5 * value * (1.0 + lax.erf(value * math.sqrt(0.5)))

    for pair in range(PAIRS):
        for tile in range(2):
            lanes = slice(tile * LANES, (tile + 1) * LANES)
            one = gelu(arrived_ref[0, 2 * tile, pair, :lon_cols].astype(jnp.float32))
            two = gelu(arrived_ref[0, 2 * tile + 1, pair, :lon_cols].astype(jnp.float32))
            for row, value in ((2 * pair, join_low(one, two)), (2 * pair + 1, join_high(one, two))):
                held = fields_ref[row, :, lanes].astype(jnp.float32)
                out_ref[row, :, lanes] = (held + value).astype(jnp.bfloat16)


def blend(arrived, fields, chunk, buffer):
    first, last = chunk
    count = last - first
    band_rows, lon_cols, channels = fields.shape
    arrived = arrived.reshape(QUARTERS, QUARTERS, count * PAIRS, LON_PAD, LANES)
    held = pl.BlockSpec((UNIT, lon_cols, channels), lambda q, u: (q * UNITS + first + u, 0, 0))
    return call(
        blend_kernel,
        "blend",
        60 * count * UNIT * QUARTERS * lon_cols * channels,
        6 * count * UNIT * QUARTERS * lon_cols * channels,
        operands=[arrived, fields],
        vmem=LESS_VMEM,
        aliases=[] if buffer is None else [buffer],
        grid=(QUARTERS, count),
        in_specs=[
            pl.BlockSpec(
                (1, QUARTERS, PAIRS, LON_PAD, LANES),
                lambda q, u: (q, 0, u, 0, 0),
            ),
            pl.BlockSpec(held.block_shape, held.index_map),
        ],
        out_specs=held,
        out_shape=jax.ShapeDtypeStruct(fields.shape, fields.dtype),
    )


def legendre_kernel(degrees, order_ref, start_ref, lat_ref, out_ref, state, rows):
    tiles = ROWS // LANES
    order = order_ref[...]

    @pl.when(pl.program_id(0) == 0)
    def _():
        for tile in range(tiles):
            lanes = slice(tile * LANES, (tile + 1) * LANES)
            state[0, :, lanes] = jnp.zeros_like(order)
            state[1, :, lanes] = jnp.ones_like(order)
            state[2, :, lanes] = start_ref[...] + order * jnp.log(lat_ref[1:2, lanes])

    def pieces(index):
        return tuple(state[index, :, t * LANES : (t + 1) * LANES] for t in range(tiles))

    cosines = tuple(lat_ref[0:1, t * LANES : (t + 1) * LANES] for t in range(tiles))
    first = pl.program_id(0) * LEVEL_BLOCK

    def group(index, carry):
        previous, current, log_scale = [list(part) for part in carry]
        halves = []
        for tile in range(tiles):
            largest = jnp.maximum(jnp.abs(previous[tile]), jnp.abs(current[tile]))
            shrink = 1.0 / largest
            previous[tile] = previous[tile] * shrink
            current[tile] = current[tile] * shrink
            log_scale[tile] = log_scale[tile] + jnp.log(largest)
            halves.append(jnp.exp(0.5 * log_scale[tile]))
        for inner in range(RESCALE):
            level = (first + index * RESCALE + inner).astype(jnp.float32)
            square = (level - 1.0) * (level - 1.0)
            upper = jnp.sqrt(
                jnp.maximum(4.0 * level * level - 1.0, 0.0)
                / jnp.maximum(level * level - order * order, 1.0)
            )
            lower = jnp.sqrt(
                jnp.maximum(square - order * order, 0.0) / jnp.maximum(4.0 * square - 1.0, 1.0)
            )
            moving = level > order
            shown = jnp.logical_and(level >= order, level < degrees)
            row = pl.multiple_of((index * RESCALE + inner) * 8, 8)
            for tile in range(tiles):
                advanced = upper * (cosines[tile] * current[tile] - lower * previous[tile])
                previous[tile] = jnp.where(moving, current[tile], previous[tile])
                current[tile] = jnp.where(moving, advanced, current[tile])
                value = (current[tile] * halves[tile]) * halves[tile]
                rows[tile, pl.ds(row, 8), :] = jnp.where(shown, value, 0.0)
        return tuple(previous), tuple(current), tuple(log_scale)

    done = lax.fori_loop(
        0, LEVEL_BLOCK // RESCALE, group, (pieces(0), pieces(1), pieces(2))
    )
    for index in range(3):
        for tile in range(tiles):
            state[index, :, tile * LANES : (tile + 1) * LANES] = done[index][tile]
    for slot in range(SLOTS):
        for tile in range(tiles):
            out_ref[slot, :, tile * LANES : (tile + 1) * LANES] = rows[
                tile, pl.ds(slot, LEVEL_BLOCK, stride=8), :
            ].astype(jnp.bfloat16)


def legendre(orders, colatitude, degrees, after):
    order_col = orders.astype(jnp.float32)
    half_gamma = 0.5 * math.log(math.pi) - math.log(2.0)
    log_start = -0.5 * math.log(2.0) + 0.5 * (
        lax.lgamma(order_col + 1.5) - half_gamma - lax.lgamma(order_col + 1.0)
    )
    widen = lambda a: jnp.broadcast_to(jnp.pad(a, (0, 8 - SLOTS))[:, None], (8, LANES))
    lat = jnp.stack([jnp.cos(colatitude), jnp.sin(colatitude)])
    return call(
        functools.partial(legendre_kernel, degrees),
        "legendre",
        30 * LEVELS * 8 * ROWS,
        2 * SLOTS * LEVELS * ROWS,
        operands=[widen(order_col), widen(log_start), lat],
        after=after,
        grid=(LEVELS // LEVEL_BLOCK,),
        in_specs=[
            pl.BlockSpec((8, LANES), lambda i: (0, 0)),
            pl.BlockSpec((8, LANES), lambda i: (0, 0)),
            pl.BlockSpec((2, ROWS), lambda i: (0, 0)),
        ],
        out_specs=pl.BlockSpec((SLOTS, LEVEL_BLOCK, ROWS), lambda i: (0, i, 0)),
        out_shape=jax.ShapeDtypeStruct((SLOTS, LEVELS, ROWS), jnp.bfloat16),
        scratch_shapes=[
            pltpu.VMEM((3, 8, ROWS), jnp.float32),
            pltpu.VMEM((ROWS // LANES, LEVEL_BLOCK * 8, LANES), jnp.float32),
        ],
    )


def sine_turn(turn):
    angle = turn * (2.0 * math.pi)
    square = angle * angle
    total = jnp.full_like(angle, -1.0 / math.factorial(11))
    for power, sign in ((9, 1.0), (7, -1.0), (5, 1.0), (3, -1.0), (1, 1.0)):
        total = total * square + sign / math.factorial(power)
    return total * angle


def fourier_kernel(lon_total, first_slot, list_ref, count_ref, longitude_ref, out_ref):
    owners = count_ref.shape[1]
    modes = list_ref.shape[1]
    tiles = longitude_ref.shape[1] // LANES
    slot = first_slot + pl.program_id(0)
    row = lax.broadcasted_iota(jnp.int32, (owners, owners), 0)
    column = lax.broadcasted_iota(jnp.int32, (owners, owners), 1)
    counts = count_ref[...]
    start = jnp.sum(jnp.where(column < row, counts, 0.0), axis=1, keepdims=True)
    count = jnp.sum(jnp.where(column == row, counts, 0.0), axis=1, keepdims=True)
    mode = lax.broadcasted_iota(jnp.int32, (owners, modes), 1).astype(jnp.float32)
    found = mode == start + slot.astype(jnp.float32)
    order = jnp.sum(jnp.where(found, list_ref[...], 0.0), axis=1, keepdims=True)
    order = jnp.where(slot.astype(jnp.float32) < count, order, -1.0)
    order = jnp.broadcast_to(order, (owners, LANES))
    rest = order - 4.0 * jnp.floor(order * 0.25)
    quarter_cosine = jnp.where(rest == 0.0, 1.0, 0.0) - jnp.where(rest == 2.0, 1.0, 0.0)
    quarter_sine = jnp.where(rest == 1.0, 1.0, 0.0) - jnp.where(rest == 3.0, 1.0, 0.0)
    for tile in range(tiles // 4):
        longitude = longitude_ref[:, tile * LANES : (tile + 1) * LANES]
        product = order * longitude
        wrapped = product - lon_total * jnp.floor(product * (1.0 / lon_total) + 0.5)
        turn = wrapped * (1.0 / lon_total)
        size = jnp.abs(turn)
        cosine = sine_turn(0.25 - jnp.minimum(size, 0.5))
        folded = jnp.where(size > 0.25, jnp.where(turn < 0, -0.5, 0.5) - turn, turn)
        live = jnp.logical_and(order >= 0.0, longitude >= 0.0)
        cosine = jnp.where(live, cosine, 0.0)
        sine = jnp.where(live, -sine_turn(folded), 0.0)
        for quarter in range(4):
            place = quarter * (tiles // 4) + tile
            lanes = slice(place * LANES, (place + 1) * LANES)
            out_ref[0, 0, :, lanes] = cosine.astype(jnp.bfloat16)
            out_ref[0, 1, :, lanes] = sine.astype(jnp.bfloat16)
            cosine, sine = (
                quarter_cosine * cosine + quarter_sine * sine,
                quarter_cosine * sine - quarter_sine * cosine,
            )


def fourier_table(column_list, column_counts, slots, lon_devices, lon_cols, after=()):
    start, stop = slots
    owners = column_counts.shape[0]
    modes = -(-column_list.shape[0] // LANES) * LANES
    place = jnp.arange(lon_devices * LON_PAD, dtype=jnp.int32)
    block, inside = place // LON_PAD, place % LON_PAD
    longitude = jnp.where(inside < lon_cols, block * lon_cols + inside, -1)
    shape = (stop - start, 2, owners, place.size)
    return call(
        functools.partial(fourier_kernel, lon_devices * lon_cols, start),
        "fourier",
        20 * math.prod(shape),
        2 * math.prod(shape),
        operands=[
            jnp.pad(column_list, (0, modes - column_list.shape[0])).astype(jnp.float32)[None, :],
            column_counts.astype(jnp.float32)[None, :],
            longitude.astype(jnp.float32)[None, :],
        ],
        after=after,
        grid=(stop - start,),
        in_specs=[
            pl.BlockSpec((1, modes), lambda s: (0, 0)),
            pl.BlockSpec((1, owners), lambda s: (0, 0)),
            pl.BlockSpec((1, place.size), lambda s: (0, 0)),
        ],
        out_specs=pl.BlockSpec((1, *shape[1:]), lambda s: (s, 0, 0, 0)),
        out_shape=jax.ShapeDtypeStruct(shape, jnp.bfloat16),
    )


def regroup(array, axis):
    shape = array.shape
    split = shape[:axis] + (2, QUARTERS, HALF) + shape[axis + 1 :]
    return jnp.swapaxes(array.reshape(split), axis, axis + 1).reshape(shape)


def complex_block(mix_weight):
    top_half = jnp.concatenate([mix_weight[0], mix_weight[1]], axis=1)
    bottom_half = jnp.concatenate([-mix_weight[1], mix_weight[0]], axis=1)
    return jnp.concatenate([top_half, bottom_half], axis=0)


def exchange(array, axes):
    flat = array.reshape(array.shape[0], -1, LANES)
    flat = lax.all_to_all(flat, axes, split_axis=0, concat_axis=0, tiled=True)
    return flat.reshape(array.shape)


def shards(fields, spectral_gain, mix_weight, column_list, column_counts):
    band_rows, lon_cols, channels = fields.shape
    lat_devices = lax.axis_size("lat")
    lon_devices = lax.axis_size("lon")
    owners = lat_devices * lon_devices
    lat_total = band_rows * lat_devices
    lon_total = lon_cols * lon_devices
    degrees = spectral_gain.shape[0]
    mode_count = column_list.shape[0]

    run_ends = jnp.cumsum(column_counts)
    starts = run_ends - column_counts
    offsets = jnp.arange(SLOTS, dtype=jnp.int32)
    positions = jnp.minimum(starts[None, :] + offsets[:, None], mode_count - 1)
    matches = positions[:, :, None] == jnp.arange(mode_count, dtype=jnp.int32)
    slot_orders = jnp.sum(jnp.where(matches, column_list, 0), axis=2)
    owner_index = lax.axis_index(("lat", "lon"))
    own_orders = lax.dynamic_slice_in_dim(slot_orders, owner_index, 1, axis=1)[:, 0]
    padded = jnp.arange(ROWS, dtype=jnp.int32)
    band, inside = padded // (ROWS // lat_devices), padded % (ROWS // lat_devices)
    row = (band * band_rows + jnp.minimum(inside, band_rows - 1)).astype(jnp.float32)
    colatitude = math.pi * (row + 0.5) / lat_total

    group = lax.axis_index("lon") // QUARTERS
    mine = jnp.arange(UNITS * UNIT, dtype=jnp.int32) + group * (UNITS * UNIT)
    mine = (lax.axis_index("lat") * band_rows + mine).astype(jnp.float32)
    weights = math.pi / lat_total * jnp.sin(math.pi * (mine + 0.5) / lat_total)
    weights = jnp.repeat(weights.reshape(UNITS, 1, UNIT), HALF, axis=2)
    gain = spectral_gain.reshape(degrees, 2 * channels)
    mixing = regroup(regroup(complex_block(mix_weight), 0), 1)

    def fourier(slots, after=()):
        return fourier_table(column_list, column_counts, slots, lon_devices, lon_cols, after)

    def turned(table, slots):
        factor = jnp.where(slot_orders[slice(*slots)] == 0, 1.0, 2.0).astype(jnp.bfloat16)
        return (table * factor[:, None, :, None]).reshape(-1, lon_devices * LON_PAD).T

    early, late = SLOT_CHUNKS
    early_table = fourier(early)
    gathered = exchange(pack(fields, (early_table, weights)), "lon")
    send = forward(gathered, early_table, weights, early)
    early_arrived = exchange(send, ("lat", "lon"))
    late_table = fourier(late, (send,))
    send = forward(gathered, late_table, weights, late)
    late_arrived = exchange(send, ("lat", "lon"))
    associated = legendre(own_orders, colatitude, degrees, (send,))
    early_spectrum, send = middle(early_arrived, associated, gain, mixing, early)
    early_landed = exchange(send, ("lat", "lon"))
    early_back, late_back = turned(early_table, early), turned(late_table, late)
    late_spectrum, send = middle(
        late_arrived, associated, gain, mixing, late, (early_back, late_back)
    )
    late_landed = exchange(send, ("lat", "lon"))
    spectrum = jnp.concatenate([early_spectrum, late_spectrum])
    partials = [inverse(early_landed, early_back, chunk, lon_total) for chunk in HOME_CHUNKS]
    spectrum = spectrum.reshape(1, SLOTS, degrees, 2, channels)
    sends = [
        inverse(late_landed, late_back, chunk, lon_total, partial, (spectrum,))
        for chunk, partial in zip(HOME_CHUNKS, partials)
    ]
    homes = [exchange(send, "lon") for send in sends]
    blended = None
    for chunk, home in zip(HOME_CHUNKS, homes):
        blended = blend(home, fields, chunk, blended)
    return blended, spectrum


def solution(mesh):
    placed = (P("lat", "lon", None), P(), P(), P(), P())
    return jax.shard_map(
        shards,
        mesh=mesh,
        in_specs=placed,
        out_specs=(P("lat", "lon", None), P(("lat", "lon"), None, None, None, None)),
        check_vma=False,
    )
```

```python
import functools
import math

import jax
import jax.numpy as jnp
from jax import lax
from jax.experimental import pallas as pl
from jax.experimental.pallas import tpu as pltpu
from jax.sharding import PartitionSpec as P

QUARTERS = 4
UNIT = 8
UNITS = 3
PAIRS = UNIT // 2
LON_PAD = 96
HALF = 64
LANES = 128
SLOTS = 7
LEVELS = 768
ROWS = 768
HOME_CHUNKS = ((0, 3),)
SLOT_CHUNKS = ((0, 3), (3, 7))
VMEM = 60
SEND_VMEM = 54
LESS_VMEM = 28
LEVEL_BLOCK = 128
RESCALE = 8


def call(
    kernel, name, flops, moved, operands, in_specs, after=(), aliases=(), vmem=VMEM, **kwargs
):
    known = len(operands)
    extra = list(after) + list(aliases)

    def body(*refs):
        kernel(*refs[:known], *refs[known + len(extra) :])

    return pl.pallas_call(
        body,
        name=name,
        compiler_params=pltpu.CompilerParams(vmem_limit_bytes=vmem * 1024 * 1024),
        cost_estimate=pl.CostEstimate(flops=flops, bytes_accessed=moved, transcendentals=0),
        in_specs=list(in_specs) + [pl.BlockSpec(memory_space=pl.ANY)] * len(extra),
        input_output_aliases={known + len(after) + i: i for i in range(len(aliases))},
        **kwargs,
    )(*operands, *extra)


def low_half():
    return lax.broadcasted_iota(jnp.int32, (1, LANES), 1) < HALF


def swap(value):
    return pltpu.roll(value, HALF, value.ndim - 1)


def join_low(first, second):
    return jnp.where(low_half(), first, swap(second))


def join_high(first, second):
    return jnp.where(low_half(), swap(first), second)


def pack_kernel(band_rows, fields_ref, out_ref):
    rows, lon_cols = fields_ref.shape[:2]
    base = pl.program_id(0) * rows
    out_ref[0, :, :, lon_cols:, :] = jnp.zeros(
        (QUARTERS, rows // 2, LON_PAD - lon_cols, LANES), jnp.bfloat16
    )

    def one_pair(pair, carry):
        first = fields_ref[2 * pair].astype(jnp.float32)
        second = fields_ref[2 * pair + 1].astype(jnp.float32)
        first = jnp.where(base + 2 * pair < band_rows, first, 0.0)
        second = jnp.where(base + 2 * pair + 1 < band_rows, second, 0.0)
        for tile in range(2):
            lanes = slice(tile * LANES, (tile + 1) * LANES)
            one, two = first[:, lanes], second[:, lanes]
            out_ref[0, 2 * tile, pair, :lon_cols] = join_low(one, two).astype(jnp.bfloat16)
            out_ref[0, 2 * tile + 1, pair, :lon_cols] = join_high(one, two).astype(jnp.bfloat16)
        return carry

    lax.fori_loop(0, rows // 2, one_pair, 0)


def pack(fields, after):
    band_rows, lon_cols, channels = fields.shape
    rows = UNITS * UNIT
    out = call(
        functools.partial(pack_kernel, band_rows),
        "pack",
        0,
        4 * rows * QUARTERS * LON_PAD * channels,
        operands=[fields],
        after=after,
        vmem=SEND_VMEM,
        grid=(QUARTERS,),
        in_specs=[pl.BlockSpec((rows, lon_cols, channels), lambda q: (q, 0, 0))],
        out_specs=pl.BlockSpec(
            (1, QUARTERS, rows // 2, LON_PAD, LANES), lambda q: (q, 0, 0, 0, 0)
        ),
        out_shape=jax.ShapeDtypeStruct(
            (QUARTERS, QUARTERS, rows // 2, LON_PAD, LANES), jnp.bfloat16
        ),
    )
    return out.reshape(QUARTERS * QUARTERS, rows // 2, LON_PAD, LANES)


def forward_kernel(arrived_ref, table_ref, weight_ref, out_ref, matrix, turned):
    sources = arrived_ref.shape[0]
    slots, _, owners, longitudes = table_ref.shape
    for pair in range(PAIRS):
        matrix[:, pair * LANES : (pair + 1) * LANES] = arrived_ref[:, pair].reshape(
            sources * LON_PAD, LANES
        )
    weights = weight_ref[0]

    for slot in range(slots):
        table = table_ref[slot].reshape(2 * owners, longitudes)
        summed = jnp.dot(table, matrix[...], preferred_element_type=jnp.float32)
        for pair in range(PAIRS):
            lanes = slice(pair * LANES, (pair + 1) * LANES)
            real = summed[:owners, lanes] * weights[:, lanes]
            imag = summed[owners:, lanes] * weights[:, lanes]
            turned[slot, pl.ds(2 * pair, owners, stride=UNIT), :] = join_low(real, imag)
            turned[slot, pl.ds(2 * pair + 1, owners, stride=UNIT), :] = join_high(real, imag)
        out_ref[:, slot, 0] = turned[slot].reshape(owners, UNIT, LANES).astype(jnp.bfloat16)


def forward(arrived, table, weights, slots, after=()):
    start, stop = slots
    sources = arrived.shape[0]
    owners, longitudes = table.shape[2:]
    work = UNITS * (stop - start)
    return call(
        forward_kernel,
        "forward",
        2 * work * 2 * owners * longitudes * PAIRS * LANES,
        2 * (arrived.size + (stop - start) * 2 * owners * longitudes),
        operands=[arrived, table, weights],
        after=after,
        vmem=SEND_VMEM,
        grid=(UNITS,),
        in_specs=[
            pl.BlockSpec((sources, PAIRS, LON_PAD, LANES), lambda u: (0, u, 0, 0)),
            pl.BlockSpec((stop - start, 2, owners, longitudes), lambda u: (0, 0, 0, 0)),
            pl.BlockSpec((1, 1, PAIRS * LANES), lambda u: (u, 0, 0)),
        ],
        out_specs=pl.BlockSpec(
            (owners, stop - start, 1, UNIT, LANES), lambda u: (0, 0, u, 0, 0)
        ),
        out_shape=jax.ShapeDtypeStruct((owners, stop - start, UNITS, UNIT, LANES), jnp.bfloat16),
        scratch_shapes=[
            pltpu.VMEM((sources * LON_PAD, PAIRS * LANES), jnp.bfloat16),
            pltpu.VMEM((stop - start, owners * UNIT, LANES), jnp.float32),
        ],
    )


def middle_kernel(arrived_ref, table_ref, gain_ref, mixing_ref, spectrum_ref, out_ref):
    degrees, width = gain_ref.shape
    arrived = arrived_ref[:, 0].astype(jnp.float32)
    groups = arrived.shape[0] // QUARTERS
    arrived = arrived.reshape(groups, QUARTERS, UNITS * UNIT, LANES)
    columns = jnp.concatenate(
        [
            arrived[:, quarter].reshape(ROWS, LANES).astype(jnp.bfloat16)
            for quarter in range(QUARTERS)
        ],
        axis=1,
    )
    spectra = jnp.dot(table_ref[0, :degrees], columns, preferred_element_type=jnp.float32)
    parts = []
    for quarter in range(QUARTERS):
        tile = quarter // 2
        real = gain_ref[:, tile * LANES : (tile + 1) * LANES]
        imag = gain_ref[:, (2 + tile) * LANES : (3 + tile) * LANES]
        join = join_high if quarter % 2 else join_low
        piece = spectra[:, quarter * LANES : (quarter + 1) * LANES]
        piece = join(real, real) * piece + join(-imag, imag) * swap(piece)
        parts.append(piece.astype(jnp.bfloat16))
    scaled = jnp.concatenate(parts, axis=1)
    mixed = jnp.dot(scaled, mixing_ref[...], preferred_element_type=jnp.float32)
    pieces = [mixed[:, q * LANES : (q + 1) * LANES] for q in range(QUARTERS)]
    for tile in range(2):
        one, two = pieces[2 * tile], pieces[2 * tile + 1]
        lanes = slice(tile * LANES, (tile + 1) * LANES)
        spectrum_ref[0, :, lanes] = join_low(one, two).astype(jnp.bfloat16)
        lanes = slice((2 + tile) * LANES, (3 + tile) * LANES)
        spectrum_ref[0, :, lanes] = join_high(one, two).astype(jnp.bfloat16)
    filled = jnp.concatenate(
        [mixed.astype(jnp.bfloat16), jnp.zeros((LEVELS - degrees, width), jnp.bfloat16)], axis=0
    )
    returned = lax.dot_general(
        table_ref[0], filled, (((0,), (0,)), ((), ())), preferred_element_type=jnp.float32
    )
    for quarter in range(QUARTERS):
        piece = returned[:, quarter * LANES : (quarter + 1) * LANES]
        out_ref[:, quarter, 0] = piece.reshape(groups, UNITS, UNIT, LANES).astype(jnp.bfloat16)


def middle(arrived, table, gain, mixing, slots, after=()):
    start, stop = slots
    owners = arrived.shape[0]
    groups = owners // QUARTERS
    degrees, width = gain.shape
    spectrum, out = call(
        middle_kernel,
        "middle",
        2 * (stop - start) * LEVELS * width * (2 * ROWS + width),
        (stop - start) * (4 * LEVELS * ROWS + 6 * LEVELS * width),
        operands=[arrived, table, gain, mixing],
        after=after,
        grid=(stop - start,),
        in_specs=[
            pl.BlockSpec((owners, 1, UNITS, UNIT, LANES), lambda s: (0, s, 0, 0, 0)),
            pl.BlockSpec((1, LEVELS, ROWS), lambda s: (start + s, 0, 0)),
            pl.BlockSpec(gain.shape, lambda s: (0, 0)),
            pl.BlockSpec(mixing.shape, lambda s: (0, 0)),
        ],
        out_specs=[
            pl.BlockSpec((1, degrees, width), lambda s: (s, 0, 0)),
            pl.BlockSpec((groups, QUARTERS, 1, UNITS, UNIT, LANES), lambda s: (0, 0, s, 0, 0, 0)),
        ],
        out_shape=[
            jax.ShapeDtypeStruct((stop - start, degrees, width), jnp.bfloat16),
            jax.ShapeDtypeStruct(
                (groups, QUARTERS, stop - start, UNITS, UNIT, LANES), jnp.bfloat16
            ),
        ],
    )
    return spectrum, out.reshape(owners, stop - start, UNITS, UNIT, LANES)


def inverse_kernel(scale, has_partial, *refs):
    arrived_ref, table_ref = refs[:2]
    partial_ref = refs[2] if has_partial else None
    out_ref, matrix, wide = refs[-3:]
    owners, slots = arrived_ref.shape[:2]

    for slot in range(slots):
        rows = slice(slot * 2 * owners, (slot * 2 + 1) * owners)
        more = slice((slot * 2 + 1) * owners, (slot * 2 + 2) * owners)
        wide[slot] = arrived_ref[:, slot, 0].astype(jnp.float32).reshape(owners * UNIT, LANES)
        for pair in range(PAIRS):
            one = wide[slot, pl.ds(2 * pair, owners, stride=UNIT), :]
            two = wide[slot, pl.ds(2 * pair + 1, owners, stride=UNIT), :]
            lanes = slice(pair * LANES, (pair + 1) * LANES)
            matrix[rows, lanes] = join_low(one, two).astype(jnp.bfloat16)
            matrix[more, lanes] = join_high(one, two).astype(jnp.bfloat16)
    blocks = 4
    for first in range(0, table_ref.shape[0], blocks * LON_PAD):
        rows = slice(first, first + blocks * LON_PAD)
        summed = jnp.dot(table_ref[rows], matrix[...], preferred_element_type=jnp.float32)
        if not has_partial:
            out_ref[0, rows] = summed
            continue
        summed = ((summed + partial_ref[0, rows]) * scale).astype(jnp.bfloat16)
        place = slice(first // LON_PAD, first // LON_PAD + blocks)
        for pair in range(PAIRS):
            lanes = slice(pair * LANES, (pair + 1) * LANES)
            out_ref[place, pair] = summed[:, lanes].reshape(blocks, LON_PAD, LANES)


def inverse(arrived, table, chunk, lon_total, partial=None, after=()):
    first, last = chunk
    count = last - first
    owners, slots = arrived.shape[:2]
    targets = table.shape[0] // LON_PAD
    has_partial = partial is not None
    summed = pl.BlockSpec((1, table.shape[0], PAIRS * LANES), lambda u: (u, 0, 0))
    if has_partial:
        spec = pl.BlockSpec((targets, PAIRS, LON_PAD, LANES), lambda u: (0, u, 0, 0))
        shape = jax.ShapeDtypeStruct((targets, count * PAIRS, LON_PAD, LANES), jnp.bfloat16)
    else:
        spec = summed
        shape = jax.ShapeDtypeStruct((count, table.shape[0], PAIRS * LANES), jnp.float32)
    return call(
        functools.partial(inverse_kernel, 1.0 / lon_total, has_partial),
        "inverse",
        2 * count * table.size * PAIRS * LANES,
        2 * 2 * table.size,
        operands=[arrived, table] + ([partial] if has_partial else []),
        after=after,
        vmem=SEND_VMEM if has_partial else VMEM,
        grid=(count,),
        in_specs=[
            pl.BlockSpec((owners, slots, 1, UNIT, LANES), lambda u: (0, 0, first + u, 0, 0)),
            pl.BlockSpec(table.shape, lambda u: (0, 0)),
        ]
        + ([summed] if has_partial else []),
        out_specs=spec,
        out_shape=shape,
        scratch_shapes=[
            pltpu.VMEM((table.shape[1], PAIRS * LANES), jnp.bfloat16),
            pltpu.VMEM((slots, owners * UNIT, LANES), jnp.float32),
        ],
    )


def gelu(value):
    return 0.5 * value * (1.0 + lax.erf(value * math.sqrt(0.5)))


def blend_kernel(arrived_ref, fields_ref, out_ref):
    lon_cols = fields_ref.shape[1]

    for pair in range(PAIRS):
        for tile in range(2):
            lanes = slice(tile * LANES, (tile + 1) * LANES)
            one = gelu(arrived_ref[0, 2 * tile, pair, :lon_cols].astype(jnp.float32))
            two = gelu(arrived_ref[0, 2 * tile + 1, pair, :lon_cols].astype(jnp.float32))
            for row, value in ((2 * pair, join_low(one, two)), (2 * pair + 1, join_high(one, two))):
                held = fields_ref[row, :, lanes].astype(jnp.float32)
                out_ref[row, :, lanes] = (held + value).astype(jnp.bfloat16)


def blend(arrived, fields, chunk, buffer):
    first, last = chunk
    count = last - first
    band_rows, lon_cols, channels = fields.shape
    arrived = arrived.reshape(QUARTERS, QUARTERS, count * PAIRS, LON_PAD, LANES)
    held = pl.BlockSpec((UNIT, lon_cols, channels), lambda q, u: (q * UNITS + first + u, 0, 0))
    return call(
        blend_kernel,
        "blend",
        60 * count * UNIT * QUARTERS * lon_cols * channels,
        6 * count * UNIT * QUARTERS * lon_cols * channels,
        operands=[arrived, fields],
        vmem=LESS_VMEM,
        aliases=[] if buffer is None else [buffer],
        grid=(QUARTERS, count),
        in_specs=[
            pl.BlockSpec(
                (1, QUARTERS, PAIRS, LON_PAD, LANES),
                lambda q, u: (q, 0, u, 0, 0),
            ),
            pl.BlockSpec(held.block_shape, held.index_map),
        ],
        out_specs=held,
        out_shape=jax.ShapeDtypeStruct(fields.shape, fields.dtype),
    )


def legendre_kernel(degrees, order_ref, start_ref, lat_ref, out_ref, state, rows):
    tiles = ROWS // LANES
    order = order_ref[...]

    @pl.when(pl.program_id(0) == 0)
    def _():
        for tile in range(tiles):
            lanes = slice(tile * LANES, (tile + 1) * LANES)
            state[0, :, lanes] = jnp.zeros_like(order)
            state[1, :, lanes] = jnp.ones_like(order)
            state[2, :, lanes] = start_ref[...] + order * jnp.log(lat_ref[1:2, lanes])

    def pieces(index):
        return tuple(state[index, :, t * LANES : (t + 1) * LANES] for t in range(tiles))

    cosines = tuple(lat_ref[0:1, t * LANES : (t + 1) * LANES] for t in range(tiles))
    first = pl.program_id(0) * LEVEL_BLOCK

    def group(index, carry):
        previous, current, log_scale = [list(part) for part in carry]
        halves = []
        for tile in range(tiles):
            largest = jnp.maximum(jnp.abs(previous[tile]), jnp.abs(current[tile]))
            shrink = 1.0 / largest
            previous[tile] = previous[tile] * shrink
            current[tile] = current[tile] * shrink
            log_scale[tile] = log_scale[tile] + jnp.log(largest)
            halves.append(jnp.exp(0.5 * log_scale[tile]))
        for inner in range(RESCALE):
            level = (first + index * RESCALE + inner).astype(jnp.float32)
            square = (level - 1.0) * (level - 1.0)
            upper = jnp.sqrt(
                jnp.maximum(4.0 * level * level - 1.0, 0.0)
                / jnp.maximum(level * level - order * order, 1.0)
            )
            lower = jnp.sqrt(
                jnp.maximum(square - order * order, 0.0) / jnp.maximum(4.0 * square - 1.0, 1.0)
            )
            moving = level > order
            shown = jnp.logical_and(level >= order, level < degrees)
            row = pl.multiple_of((index * RESCALE + inner) * 8, 8)
            for tile in range(tiles):
                advanced = upper * (cosines[tile] * current[tile] - lower * previous[tile])
                previous[tile] = jnp.where(moving, current[tile], previous[tile])
                current[tile] = jnp.where(moving, advanced, current[tile])
                value = (current[tile] * halves[tile]) * halves[tile]
                rows[tile, pl.ds(row, 8), :] = jnp.where(shown, value, 0.0)
        return tuple(previous), tuple(current), tuple(log_scale)

    done = lax.fori_loop(
        0, LEVEL_BLOCK // RESCALE, group, (pieces(0), pieces(1), pieces(2))
    )
    for index in range(3):
        for tile in range(tiles):
            state[index, :, tile * LANES : (tile + 1) * LANES] = done[index][tile]
    for slot in range(SLOTS):
        for tile in range(tiles):
            out_ref[slot, :, tile * LANES : (tile + 1) * LANES] = rows[
                tile, pl.ds(slot, LEVEL_BLOCK, stride=8), :
            ].astype(jnp.bfloat16)


def legendre(orders, colatitude, degrees, after):
    order_col = orders.astype(jnp.float32)
    half_gamma = 0.5 * math.log(math.pi) - math.log(2.0)
    log_start = -0.5 * math.log(2.0) + 0.5 * (
        lax.lgamma(order_col + 1.5) - half_gamma - lax.lgamma(order_col + 1.0)
    )
    widen = lambda a: jnp.broadcast_to(jnp.pad(a, (0, 8 - SLOTS))[:, None], (8, LANES))
    lat = jnp.stack([jnp.cos(colatitude), jnp.sin(colatitude)])
    return call(
        functools.partial(legendre_kernel, degrees),
        "legendre",
        30 * LEVELS * 8 * ROWS,
        2 * SLOTS * LEVELS * ROWS,
        operands=[widen(order_col), widen(log_start), lat],
        after=after,
        grid=(LEVELS // LEVEL_BLOCK,),
        in_specs=[
            pl.BlockSpec((8, LANES), lambda i: (0, 0)),
            pl.BlockSpec((8, LANES), lambda i: (0, 0)),
            pl.BlockSpec((2, ROWS), lambda i: (0, 0)),
        ],
        out_specs=pl.BlockSpec((SLOTS, LEVEL_BLOCK, ROWS), lambda i: (0, i, 0)),
        out_shape=jax.ShapeDtypeStruct((SLOTS, LEVELS, ROWS), jnp.bfloat16),
        scratch_shapes=[
            pltpu.VMEM((3, 8, ROWS), jnp.float32),
            pltpu.VMEM((ROWS // LANES, LEVEL_BLOCK * 8, LANES), jnp.float32),
        ],
    )


def sine_turn(turn):
    angle = turn * (2.0 * math.pi)
    square = angle * angle
    total = jnp.full_like(angle, -1.0 / math.factorial(11))
    for power, sign in ((9, 1.0), (7, -1.0), (5, 1.0), (3, -1.0), (1, 1.0)):
        total = total * square + sign / math.factorial(power)
    return total * angle


def fourier_kernel(lon_total, first_slot, list_ref, count_ref, longitude_ref, out_ref):
    owners = count_ref.shape[1]
    modes = list_ref.shape[1]
    tiles = longitude_ref.shape[1] // LANES
    slot = first_slot + pl.program_id(0)
    row = lax.broadcasted_iota(jnp.int32, (owners, owners), 0)
    column = lax.broadcasted_iota(jnp.int32, (owners, owners), 1)
    counts = count_ref[...].astype(jnp.float32)
    start = jnp.sum(jnp.where(column < row, counts, 0.0), axis=1, keepdims=True)
    count = jnp.sum(jnp.where(column == row, counts, 0.0), axis=1, keepdims=True)
    mode = lax.broadcasted_iota(jnp.int32, (owners, modes), 1).astype(jnp.float32)
    found = mode == start + slot.astype(jnp.float32)
    order = jnp.sum(jnp.where(found, list_ref[...].astype(jnp.float32), 0.0), axis=1, keepdims=True)
    order = jnp.where(slot.astype(jnp.float32) < count, order, -1.0)
    order = jnp.broadcast_to(order, (owners, LANES))
    rest = order - 4.0 * jnp.floor(order * 0.25)
    quarter_cosine = jnp.where(rest == 0.0, 1.0, 0.0) - jnp.where(rest == 2.0, 1.0, 0.0)
    quarter_sine = jnp.where(rest == 1.0, 1.0, 0.0) - jnp.where(rest == 3.0, 1.0, 0.0)
    for tile in range(tiles // 4):
        longitude = longitude_ref[:, tile * LANES : (tile + 1) * LANES]
        product = order * longitude
        wrapped = product - lon_total * jnp.floor(product * (1.0 / lon_total) + 0.5)
        turn = wrapped * (1.0 / lon_total)
        size = jnp.abs(turn)
        cosine = sine_turn(0.25 - jnp.minimum(size, 0.5))
        folded = jnp.where(size > 0.25, jnp.where(turn < 0, -0.5, 0.5) - turn, turn)
        live = jnp.logical_and(order >= 0.0, longitude >= 0.0)
        cosine = jnp.where(live, cosine, 0.0)
        sine = jnp.where(live, -sine_turn(folded), 0.0)
        for quarter in range(4):
            place = quarter * (tiles // 4) + tile
            lanes = slice(place * LANES, (place + 1) * LANES)
            out_ref[0, 0, :, lanes] = cosine.astype(jnp.bfloat16)
            out_ref[0, 1, :, lanes] = sine.astype(jnp.bfloat16)
            cosine, sine = (
                quarter_cosine * cosine + quarter_sine * sine,
                quarter_cosine * sine - quarter_sine * cosine,
            )


def fourier_table(column_list, column_counts, slots, lon_devices, lon_cols, after=()):
    start, stop = slots
    owners = column_counts.shape[0]
    modes = column_list.shape[0]
    place = jnp.arange(lon_devices * LON_PAD, dtype=jnp.int32)
    block, inside = place // LON_PAD, place % LON_PAD
    longitude = jnp.where(inside < lon_cols, block * lon_cols + inside, -1)
    shape = (stop - start, 2, owners, place.size)
    return call(
        functools.partial(fourier_kernel, lon_devices * lon_cols, start),
        "fourier",
        20 * math.prod(shape),
        2 * math.prod(shape),
        operands=[
            column_list[None, :],
            column_counts[None, :],
            longitude.astype(jnp.float32)[None, :],
        ],
        after=after,
        grid=(stop - start,),
        in_specs=[
            pl.BlockSpec((1, modes), lambda s: (0, 0)),
            pl.BlockSpec((1, owners), lambda s: (0, 0)),
            pl.BlockSpec((1, place.size), lambda s: (0, 0)),
        ],
        out_specs=pl.BlockSpec((1, *shape[1:]), lambda s: (s, 0, 0, 0)),
        out_shape=jax.ShapeDtypeStruct(shape, jnp.bfloat16),
    )


def regroup(array, axis):
    shape = array.shape
    split = shape[:axis] + (2, QUARTERS, HALF) + shape[axis + 1 :]
    return jnp.swapaxes(array.reshape(split), axis, axis + 1).reshape(shape)


def complex_block(mix_weight):
    top_half = jnp.concatenate([mix_weight[0], mix_weight[1]], axis=1)
    bottom_half = jnp.concatenate([-mix_weight[1], mix_weight[0]], axis=1)
    return jnp.concatenate([top_half, bottom_half], axis=0)


def exchange(array, axes):
    flat = array.reshape(array.shape[0], -1, LANES)
    flat = lax.all_to_all(flat, axes, split_axis=0, concat_axis=0, tiled=True)
    return flat.reshape(array.shape)


def shards(fields, spectral_gain, mix_weight, column_list, column_counts):
    band_rows, lon_cols, channels = fields.shape
    lat_devices = lax.axis_size("lat")
    lon_devices = lax.axis_size("lon")
    owners = lat_devices * lon_devices
    lat_total = band_rows * lat_devices
    lon_total = lon_cols * lon_devices
    degrees = spectral_gain.shape[0]
    mode_count = column_list.shape[0]

    run_ends = jnp.cumsum(column_counts)
    starts = run_ends - column_counts
    offsets = jnp.arange(SLOTS, dtype=jnp.int32)
    positions = jnp.minimum(starts[None, :] + offsets[:, None], mode_count - 1)
    matches = positions[:, :, None] == jnp.arange(mode_count, dtype=jnp.int32)
    slot_orders = jnp.sum(jnp.where(matches, column_list, 0), axis=2)
    owner_index = lax.axis_index(("lat", "lon"))
    own_orders = lax.dynamic_slice_in_dim(slot_orders, owner_index, 1, axis=1)[:, 0]
    padded = jnp.arange(ROWS, dtype=jnp.int32)
    band, inside = padded // (ROWS // lat_devices), padded % (ROWS // lat_devices)
    row = (band * band_rows + jnp.minimum(inside, band_rows - 1)).astype(jnp.float32)
    colatitude = math.pi * (row + 0.5) / lat_total

    group = lax.axis_index("lon") // QUARTERS
    mine = jnp.arange(UNITS * UNIT, dtype=jnp.int32) + group * (UNITS * UNIT)
    mine = (lax.axis_index("lat") * band_rows + mine).astype(jnp.float32)
    weights = math.pi / lat_total * jnp.sin(math.pi * (mine + 0.5) / lat_total)
    weights = jnp.repeat(weights.reshape(UNITS, 1, UNIT), HALF, axis=2)
    gain = spectral_gain.reshape(degrees, 2 * channels)
    mixing = regroup(regroup(complex_block(mix_weight), 0), 1)

    def fourier(slots, after=()):
        return fourier_table(column_list, column_counts, slots, lon_devices, lon_cols, after)

    def turned(table, slots):
        factor = jnp.where(slot_orders[slice(*slots)] == 0, 1.0, 2.0).astype(jnp.bfloat16)
        return (table * factor[:, None, :, None]).reshape(-1, lon_devices * LON_PAD).T

    early, late = SLOT_CHUNKS
    early_table = fourier(early)
    gathered = exchange(pack(fields, (early_table, weights)), "lon")
    send = forward(gathered, early_table, weights, early)
    early_arrived = exchange(send, ("lat", "lon"))
    late_table = fourier(late, (send,))
    send = forward(gathered, late_table, weights, late)
    late_arrived = exchange(send, ("lat", "lon"))
    associated = legendre(own_orders, colatitude, degrees, (send,))
    early_spectrum, send = middle(early_arrived, associated, gain, mixing, early)
    early_landed = exchange(send, ("lat", "lon"))
    early_back, late_back = turned(early_table, early), turned(late_table, late)
    late_spectrum, send = middle(
        late_arrived, associated, gain, mixing, late, (early_back, late_back)
    )
    late_landed = exchange(send, ("lat", "lon"))
    spectrum = jnp.concatenate([early_spectrum, late_spectrum])
    partials = [inverse(early_landed, early_back, chunk, lon_total) for chunk in HOME_CHUNKS]
    spectrum = spectrum.reshape(1, SLOTS, degrees, 2, channels)
    sends = [
        inverse(late_landed, late_back, chunk, lon_total, partial, (spectrum,))
        for chunk, partial in zip(HOME_CHUNKS, partials)
    ]
    homes = [exchange(send, "lon") for send in sends]
    blended = None
    for chunk, home in zip(HOME_CHUNKS, homes):
        blended = blend(home, fields, chunk, blended)
    return blended, spectrum


def solution(mesh):
    placed = (P("lat", "lon", None), P(), P(), P(), P())
    return jax.shard_map(
        shards,
        mesh=mesh,
        in_specs=placed,
        out_specs=(P("lat", "lon", None), P(("lat", "lon"), None, None, None, None)),
        check_vma=False,
    )
```

```python
import functools
import math

import jax
import jax.numpy as jnp
from jax import lax
from jax.experimental import pallas as pl
from jax.experimental.pallas import tpu as pltpu
from jax.sharding import PartitionSpec as P

QUARTERS = 4
UNIT = 8
UNITS = 3
PAIRS = UNIT // 2
LON_PAD = 96
HALF = 64
LANES = 128
SLOTS = 7
LEVELS = 768
ROWS = 768
HOME_CHUNKS = ((0, 3),)
SLOT_CHUNKS = ((0, 2), (2, 7))
VMEM = 60
SEND_VMEM = 54
LESS_VMEM = 28
LEVEL_BLOCK = 128
RESCALE = 8


def call(
    kernel, name, flops, moved, operands, in_specs, after=(), aliases=(), vmem=VMEM, **kwargs
):
    known = len(operands)
    extra = list(after) + list(aliases)

    def body(*refs):
        kernel(*refs[:known], *refs[known + len(extra) :])

    return pl.pallas_call(
        body,
        name=name,
        compiler_params=pltpu.CompilerParams(vmem_limit_bytes=vmem * 1024 * 1024),
        cost_estimate=pl.CostEstimate(flops=flops, bytes_accessed=moved, transcendentals=0),
        in_specs=list(in_specs) + [pl.BlockSpec(memory_space=pl.ANY)] * len(extra),
        input_output_aliases={known + len(after) + i: i for i in range(len(aliases))},
        **kwargs,
    )(*operands, *extra)


def low_half():
    return lax.broadcasted_iota(jnp.int32, (1, LANES), 1) < HALF


def swap(value):
    return pltpu.roll(value, HALF, value.ndim - 1)


def join_low(first, second):
    return jnp.where(low_half(), first, swap(second))


def join_high(first, second):
    return jnp.where(low_half(), swap(first), second)


def pack_kernel(band_rows, fields_ref, out_ref):
    rows, lon_cols = fields_ref.shape[:2]
    base = pl.program_id(0) * rows
    out_ref[0, :, :, lon_cols:, :] = jnp.zeros(
        (QUARTERS, rows // 2, LON_PAD - lon_cols, LANES), jnp.bfloat16
    )

    def one_pair(pair, carry):
        first = fields_ref[2 * pair].astype(jnp.float32)
        second = fields_ref[2 * pair + 1].astype(jnp.float32)
        first = jnp.where(base + 2 * pair < band_rows, first, 0.0)
        second = jnp.where(base + 2 * pair + 1 < band_rows, second, 0.0)
        for tile in range(2):
            lanes = slice(tile * LANES, (tile + 1) * LANES)
            one, two = first[:, lanes], second[:, lanes]
            out_ref[0, 2 * tile, pair, :lon_cols] = join_low(one, two).astype(jnp.bfloat16)
            out_ref[0, 2 * tile + 1, pair, :lon_cols] = join_high(one, two).astype(jnp.bfloat16)
        return carry

    lax.fori_loop(0, rows // 2, one_pair, 0)


def pack(fields, after):
    band_rows, lon_cols, channels = fields.shape
    rows = UNITS * UNIT
    out = call(
        functools.partial(pack_kernel, band_rows),
        "pack",
        0,
        4 * rows * QUARTERS * LON_PAD * channels,
        operands=[fields],
        after=after,
        vmem=SEND_VMEM,
        grid=(QUARTERS,),
        in_specs=[pl.BlockSpec((rows, lon_cols, channels), lambda q: (q, 0, 0))],
        out_specs=pl.BlockSpec(
            (1, QUARTERS, rows // 2, LON_PAD, LANES), lambda q: (q, 0, 0, 0, 0)
        ),
        out_shape=jax.ShapeDtypeStruct(
            (QUARTERS, QUARTERS, rows // 2, LON_PAD, LANES), jnp.bfloat16
        ),
    )
    return out.reshape(QUARTERS * QUARTERS, rows // 2, LON_PAD, LANES)


def forward_kernel(arrived_ref, table_ref, weight_ref, out_ref, matrix, turned):
    sources = arrived_ref.shape[0]
    slots, _, owners, longitudes = table_ref.shape
    for pair in range(PAIRS):
        matrix[:, pair * LANES : (pair + 1) * LANES] = arrived_ref[:, pair].reshape(
            sources * LON_PAD, LANES
        )
    weights = weight_ref[0]

    for slot in range(slots):
        table = table_ref[slot].reshape(2 * owners, longitudes)
        summed = jnp.dot(table, matrix[...], preferred_element_type=jnp.float32)
        for pair in range(PAIRS):
            lanes = slice(pair * LANES, (pair + 1) * LANES)
            real = summed[:owners, lanes] * weights[:, lanes]
            imag = summed[owners:, lanes] * weights[:, lanes]
            turned[slot, pl.ds(2 * pair, owners, stride=UNIT), :] = join_low(real, imag)
            turned[slot, pl.ds(2 * pair + 1, owners, stride=UNIT), :] = join_high(real, imag)
        out_ref[:, slot, 0] = turned[slot].reshape(owners, UNIT, LANES).astype(jnp.bfloat16)


def forward(arrived, table, weights, slots, after=()):
    start, stop = slots
    sources = arrived.shape[0]
    owners, longitudes = table.shape[2:]
    work = UNITS * (stop - start)
    return call(
        forward_kernel,
        "forward",
        2 * work * 2 * owners * longitudes * PAIRS * LANES,
        2 * (arrived.size + (stop - start) * 2 * owners * longitudes),
        operands=[arrived, table, weights],
        after=after,
        vmem=SEND_VMEM,
        grid=(UNITS,),
        in_specs=[
            pl.BlockSpec((sources, PAIRS, LON_PAD, LANES), lambda u: (0, u, 0, 0)),
            pl.BlockSpec((stop - start, 2, owners, longitudes), lambda u: (0, 0, 0, 0)),
            pl.BlockSpec((1, 1, PAIRS * LANES), lambda u: (u, 0, 0)),
        ],
        out_specs=pl.BlockSpec(
            (owners, stop - start, 1, UNIT, LANES), lambda u: (0, 0, u, 0, 0)
        ),
        out_shape=jax.ShapeDtypeStruct((owners, stop - start, UNITS, UNIT, LANES), jnp.bfloat16),
        scratch_shapes=[
            pltpu.VMEM((sources * LON_PAD, PAIRS * LANES), jnp.bfloat16),
            pltpu.VMEM((stop - start, owners * UNIT, LANES), jnp.float32),
        ],
    )


def middle_kernel(arrived_ref, table_ref, gain_ref, mixing_ref, spectrum_ref, out_ref):
    degrees, width = gain_ref.shape
    arrived = arrived_ref[:, 0].astype(jnp.float32)
    groups = arrived.shape[0] // QUARTERS
    arrived = arrived.reshape(groups, QUARTERS, UNITS * UNIT, LANES)
    columns = jnp.concatenate(
        [
            arrived[:, quarter].reshape(ROWS, LANES).astype(jnp.bfloat16)
            for quarter in range(QUARTERS)
        ],
        axis=1,
    )
    spectra = jnp.dot(table_ref[0, :degrees], columns, preferred_element_type=jnp.float32)
    parts = []
    for quarter in range(QUARTERS):
        tile = quarter // 2
        real = gain_ref[:, tile * LANES : (tile + 1) * LANES]
        imag = gain_ref[:, (2 + tile) * LANES : (3 + tile) * LANES]
        join = join_high if quarter % 2 else join_low
        piece = spectra[:, quarter * LANES : (quarter + 1) * LANES]
        piece = join(real, real) * piece + join(-imag, imag) * swap(piece)
        parts.append(piece.astype(jnp.bfloat16))
    scaled = jnp.concatenate(parts, axis=1)
    mixed = jnp.dot(scaled, mixing_ref[...], preferred_element_type=jnp.float32)
    pieces = [mixed[:, q * LANES : (q + 1) * LANES] for q in range(QUARTERS)]
    for tile in range(2):
        one, two = pieces[2 * tile], pieces[2 * tile + 1]
        lanes = slice(tile * LANES, (tile + 1) * LANES)
        spectrum_ref[0, :, lanes] = join_low(one, two).astype(jnp.bfloat16)
        lanes = slice((2 + tile) * LANES, (3 + tile) * LANES)
        spectrum_ref[0, :, lanes] = join_high(one, two).astype(jnp.bfloat16)
    filled = jnp.concatenate(
        [mixed.astype(jnp.bfloat16), jnp.zeros((LEVELS - degrees, width), jnp.bfloat16)], axis=0
    )
    returned = lax.dot_general(
        table_ref[0], filled, (((0,), (0,)), ((), ())), preferred_element_type=jnp.float32
    )
    for quarter in range(QUARTERS):
        piece = returned[:, quarter * LANES : (quarter + 1) * LANES]
        out_ref[:, quarter, 0] = piece.reshape(groups, UNITS, UNIT, LANES).astype(jnp.bfloat16)


def middle(arrived, table, gain, mixing, slots, after=()):
    start, stop = slots
    owners = arrived.shape[0]
    groups = owners // QUARTERS
    degrees, width = gain.shape
    spectrum, out = call(
        middle_kernel,
        "middle",
        2 * (stop - start) * LEVELS * width * (2 * ROWS + width),
        (stop - start) * (4 * LEVELS * ROWS + 6 * LEVELS * width),
        operands=[arrived, table, gain, mixing],
        after=after,
        grid=(stop - start,),
        in_specs=[
            pl.BlockSpec((owners, 1, UNITS, UNIT, LANES), lambda s: (0, s, 0, 0, 0)),
            pl.BlockSpec((1, LEVELS, ROWS), lambda s: (start + s, 0, 0)),
            pl.BlockSpec(gain.shape, lambda s: (0, 0)),
            pl.BlockSpec(mixing.shape, lambda s: (0, 0)),
        ],
        out_specs=[
            pl.BlockSpec((1, degrees, width), lambda s: (s, 0, 0)),
            pl.BlockSpec((groups, QUARTERS, 1, UNITS, UNIT, LANES), lambda s: (0, 0, s, 0, 0, 0)),
        ],
        out_shape=[
            jax.ShapeDtypeStruct((stop - start, degrees, width), jnp.bfloat16),
            jax.ShapeDtypeStruct(
                (groups, QUARTERS, stop - start, UNITS, UNIT, LANES), jnp.bfloat16
            ),
        ],
    )
    return spectrum, out.reshape(owners, stop - start, UNITS, UNIT, LANES)


def inverse_kernel(scale, has_partial, *refs):
    arrived_ref, table_ref = refs[:2]
    partial_ref = refs[2] if has_partial else None
    out_ref, matrix, wide = refs[-3:]
    owners, slots = arrived_ref.shape[:2]

    for slot in range(slots):
        rows = slice(slot * 2 * owners, (slot * 2 + 1) * owners)
        more = slice((slot * 2 + 1) * owners, (slot * 2 + 2) * owners)
        wide[slot] = arrived_ref[:, slot, 0].astype(jnp.float32).reshape(owners * UNIT, LANES)
        for pair in range(PAIRS):
            one = wide[slot, pl.ds(2 * pair, owners, stride=UNIT), :]
            two = wide[slot, pl.ds(2 * pair + 1, owners, stride=UNIT), :]
            lanes = slice(pair * LANES, (pair + 1) * LANES)
            matrix[rows, lanes] = join_low(one, two).astype(jnp.bfloat16)
            matrix[more, lanes] = join_high(one, two).astype(jnp.bfloat16)
    blocks = 4
    for first in range(0, table_ref.shape[0], blocks * LON_PAD):
        rows = slice(first, first + blocks * LON_PAD)
        summed = jnp.dot(table_ref[rows], matrix[...], preferred_element_type=jnp.float32)
        if not has_partial:
            out_ref[0, rows] = summed
            continue
        summed = ((summed + partial_ref[0, rows]) * scale).astype(jnp.bfloat16)
        place = slice(first // LON_PAD, first // LON_PAD + blocks)
        for pair in range(PAIRS):
            lanes = slice(pair * LANES, (pair + 1) * LANES)
            out_ref[place, pair] = summed[:, lanes].reshape(blocks, LON_PAD, LANES)


def inverse(arrived, table, chunk, lon_total, partial=None, after=()):
    first, last = chunk
    count = last - first
    owners, slots = arrived.shape[:2]
    targets = table.shape[0] // LON_PAD
    has_partial = partial is not None
    summed = pl.BlockSpec((1, table.shape[0], PAIRS * LANES), lambda u: (u, 0, 0))
    if has_partial:
        spec = pl.BlockSpec((targets, PAIRS, LON_PAD, LANES), lambda u: (0, u, 0, 0))
        shape = jax.ShapeDtypeStruct((targets, count * PAIRS, LON_PAD, LANES), jnp.bfloat16)
    else:
        spec = summed
        shape = jax.ShapeDtypeStruct((count, table.shape[0], PAIRS * LANES), jnp.float32)
    return call(
        functools.partial(inverse_kernel, 1.0 / lon_total, has_partial),
        "inverse",
        2 * count * table.size * PAIRS * LANES,
        2 * 2 * table.size,
        operands=[arrived, table] + ([partial] if has_partial else []),
        after=after,
        vmem=SEND_VMEM if has_partial else VMEM,
        grid=(count,),
        in_specs=[
            pl.BlockSpec((owners, slots, 1, UNIT, LANES), lambda u: (0, 0, first + u, 0, 0)),
            pl.BlockSpec(table.shape, lambda u: (0, 0)),
        ]
        + ([summed] if has_partial else []),
        out_specs=spec,
        out_shape=shape,
        scratch_shapes=[
            pltpu.VMEM((table.shape[1], PAIRS * LANES), jnp.bfloat16),
            pltpu.VMEM((slots, owners * UNIT, LANES), jnp.float32),
        ],
    )


def gelu(value):
    return 0.5 * value * (1.0 + lax.erf(value * math.sqrt(0.5)))


def blend_kernel(arrived_ref, fields_ref, out_ref):
    lon_cols = fields_ref.shape[1]

    for pair in range(PAIRS):
        for tile in range(2):
            lanes = slice(tile * LANES, (tile + 1) * LANES)
            one = gelu(arrived_ref[0, 2 * tile, pair, :lon_cols].astype(jnp.float32))
            two = gelu(arrived_ref[0, 2 * tile + 1, pair, :lon_cols].astype(jnp.float32))
            for row, value in ((2 * pair, join_low(one, two)), (2 * pair + 1, join_high(one, two))):
                held = fields_ref[row, :, lanes].astype(jnp.float32)
                out_ref[row, :, lanes] = (held + value).astype(jnp.bfloat16)


def blend(arrived, fields, chunk, buffer):
    first, last = chunk
    count = last - first
    band_rows, lon_cols, channels = fields.shape
    arrived = arrived.reshape(QUARTERS, QUARTERS, count * PAIRS, LON_PAD, LANES)
    held = pl.BlockSpec((UNIT, lon_cols, channels), lambda q, u: (q * UNITS + first + u, 0, 0))
    return call(
        blend_kernel,
        "blend",
        60 * count * UNIT * QUARTERS * lon_cols * channels,
        6 * count * UNIT * QUARTERS * lon_cols * channels,
        operands=[arrived, fields],
        vmem=LESS_VMEM,
        aliases=[] if buffer is None else [buffer],
        grid=(QUARTERS, count),
        in_specs=[
            pl.BlockSpec(
                (1, QUARTERS, PAIRS, LON_PAD, LANES),
                lambda q, u: (q, 0, u, 0, 0),
            ),
            pl.BlockSpec(held.block_shape, held.index_map),
        ],
        out_specs=held,
        out_shape=jax.ShapeDtypeStruct(fields.shape, fields.dtype),
    )


def legendre_kernel(degrees, order_ref, start_ref, lat_ref, out_ref, state, rows):
    tiles = ROWS // LANES
    order = order_ref[...]

    @pl.when(pl.program_id(0) == 0)
    def _():
        for tile in range(tiles):
            lanes = slice(tile * LANES, (tile + 1) * LANES)
            state[0, :, lanes] = jnp.zeros_like(order)
            state[1, :, lanes] = jnp.ones_like(order)
            state[2, :, lanes] = start_ref[...] + order * jnp.log(lat_ref[1:2, lanes])

    def pieces(index):
        return tuple(state[index, :, t * LANES : (t + 1) * LANES] for t in range(tiles))

    cosines = tuple(lat_ref[0:1, t * LANES : (t + 1) * LANES] for t in range(tiles))
    first = pl.program_id(0) * LEVEL_BLOCK

    def group(index, carry):
        previous, current, log_scale = [list(part) for part in carry]
        halves = []
        for tile in range(tiles):
            largest = jnp.maximum(jnp.abs(previous[tile]), jnp.abs(current[tile]))
            shrink = 1.0 / largest
            previous[tile] = previous[tile] * shrink
            current[tile] = current[tile] * shrink
            log_scale[tile] = log_scale[tile] + jnp.log(largest)
            halves.append(jnp.exp(0.5 * log_scale[tile]))
        for inner in range(RESCALE):
            level = (first + index * RESCALE + inner).astype(jnp.float32)
            square = (level - 1.0) * (level - 1.0)
            upper = jnp.sqrt(
                jnp.maximum(4.0 * level * level - 1.0, 0.0)
                / jnp.maximum(level * level - order * order, 1.0)
            )
            lower = jnp.sqrt(
                jnp.maximum(square - order * order, 0.0) / jnp.maximum(4.0 * square - 1.0, 1.0)
            )
            moving = level > order
            shown = jnp.logical_and(level >= order, level < degrees)
            row = pl.multiple_of((index * RESCALE + inner) * 8, 8)
            for tile in range(tiles):
                advanced = upper * (cosines[tile] * current[tile] - lower * previous[tile])
                previous[tile] = jnp.where(moving, current[tile], previous[tile])
                current[tile] = jnp.where(moving, advanced, current[tile])
                value = (current[tile] * halves[tile]) * halves[tile]
                rows[tile, pl.ds(row, 8), :] = jnp.where(shown, value, 0.0)
        return tuple(previous), tuple(current), tuple(log_scale)

    done = lax.fori_loop(
        0, LEVEL_BLOCK // RESCALE, group, (pieces(0), pieces(1), pieces(2))
    )
    for index in range(3):
        for tile in range(tiles):
            state[index, :, tile * LANES : (tile + 1) * LANES] = done[index][tile]
    for slot in range(SLOTS):
        for tile in range(tiles):
            out_ref[slot, :, tile * LANES : (tile + 1) * LANES] = rows[
                tile, pl.ds(slot, LEVEL_BLOCK, stride=8), :
            ].astype(jnp.bfloat16)


def legendre(orders, colatitude, degrees, after):
    order_col = orders.astype(jnp.float32)
    half_gamma = 0.5 * math.log(math.pi) - math.log(2.0)
    log_start = -0.5 * math.log(2.0) + 0.5 * (
        lax.lgamma(order_col + 1.5) - half_gamma - lax.lgamma(order_col + 1.0)
    )
    widen = lambda a: jnp.broadcast_to(jnp.pad(a, (0, 8 - SLOTS))[:, None], (8, LANES))
    lat = jnp.stack([jnp.cos(colatitude), jnp.sin(colatitude)])
    return call(
        functools.partial(legendre_kernel, degrees),
        "legendre",
        30 * LEVELS * 8 * ROWS,
        2 * SLOTS * LEVELS * ROWS,
        operands=[widen(order_col), widen(log_start), lat],
        after=after,
        grid=(LEVELS // LEVEL_BLOCK,),
        in_specs=[
            pl.BlockSpec((8, LANES), lambda i: (0, 0)),
            pl.BlockSpec((8, LANES), lambda i: (0, 0)),
            pl.BlockSpec((2, ROWS), lambda i: (0, 0)),
        ],
        out_specs=pl.BlockSpec((SLOTS, LEVEL_BLOCK, ROWS), lambda i: (0, i, 0)),
        out_shape=jax.ShapeDtypeStruct((SLOTS, LEVELS, ROWS), jnp.bfloat16),
        scratch_shapes=[
            pltpu.VMEM((3, 8, ROWS), jnp.float32),
            pltpu.VMEM((ROWS // LANES, LEVEL_BLOCK * 8, LANES), jnp.float32),
        ],
    )


def sine_turn(turn):
    angle = turn * (2.0 * math.pi)
    square = angle * angle
    total = jnp.full_like(angle, -1.0 / math.factorial(11))
    for power, sign in ((9, 1.0), (7, -1.0), (5, 1.0), (3, -1.0), (1, 1.0)):
        total = total * square + sign / math.factorial(power)
    return total * angle


def fourier_kernel(lon_total, first_slot, list_ref, count_ref, longitude_ref, out_ref):
    owners = count_ref.shape[1]
    modes = list_ref.shape[1]
    tiles = longitude_ref.shape[1] // LANES
    slot = first_slot + pl.program_id(0)
    row = lax.broadcasted_iota(jnp.int32, (owners, owners), 0)
    column = lax.broadcasted_iota(jnp.int32, (owners, owners), 1)
    counts = count_ref[...].astype(jnp.float32)
    start = jnp.sum(jnp.where(column < row, counts, 0.0), axis=1, keepdims=True)
    count = jnp.sum(jnp.where(column == row, counts, 0.0), axis=1, keepdims=True)
    mode = lax.broadcasted_iota(jnp.int32, (owners, modes), 1).astype(jnp.float32)
    found = mode == start + slot.astype(jnp.float32)
    order = jnp.sum(jnp.where(found, list_ref[...].astype(jnp.float32), 0.0), axis=1, keepdims=True)
    order = jnp.where(slot.astype(jnp.float32) < count, order, -1.0)
    order = jnp.broadcast_to(order, (owners, LANES))
    rest = order - 4.0 * jnp.floor(order * 0.25)
    quarter_cosine = jnp.where(rest == 0.0, 1.0, 0.0) - jnp.where(rest == 2.0, 1.0, 0.0)
    quarter_sine = jnp.where(rest == 1.0, 1.0, 0.0) - jnp.where(rest == 3.0, 1.0, 0.0)
    for tile in range(tiles // 4):
        longitude = longitude_ref[:, tile * LANES : (tile + 1) * LANES]
        product = order * longitude
        wrapped = product - lon_total * jnp.floor(product * (1.0 / lon_total) + 0.5)
        turn = wrapped * (1.0 / lon_total)
        size = jnp.abs(turn)
        cosine = sine_turn(0.25 - jnp.minimum(size, 0.5))
        folded = jnp.where(size > 0.25, jnp.where(turn < 0, -0.5, 0.5) - turn, turn)
        live = jnp.logical_and(order >= 0.0, longitude >= 0.0)
        cosine = jnp.where(live, cosine, 0.0)
        sine = jnp.where(live, -sine_turn(folded), 0.0)
        for quarter in range(4):
            place = quarter * (tiles // 4) + tile
            lanes = slice(place * LANES, (place + 1) * LANES)
            out_ref[0, 0, :, lanes] = cosine.astype(jnp.bfloat16)
            out_ref[0, 1, :, lanes] = sine.astype(jnp.bfloat16)
            cosine, sine = (
                quarter_cosine * cosine + quarter_sine * sine,
                quarter_cosine * sine - quarter_sine * cosine,
            )


def fourier_table(column_list, column_counts, slots, lon_devices, lon_cols, after=()):
    start, stop = slots
    owners = column_counts.shape[0]
    modes = column_list.shape[0]
    place = jnp.arange(lon_devices * LON_PAD, dtype=jnp.int32)
    block, inside = place // LON_PAD, place % LON_PAD
    longitude = jnp.where(inside < lon_cols, block * lon_cols + inside, -1)
    shape = (stop - start, 2, owners, place.size)
    return call(
        functools.partial(fourier_kernel, lon_devices * lon_cols, start),
        "fourier",
        20 * math.prod(shape),
        2 * math.prod(shape),
        operands=[
            column_list[None, :],
            column_counts[None, :],
            longitude.astype(jnp.float32)[None, :],
        ],
        after=after,
        grid=(stop - start,),
        in_specs=[
            pl.BlockSpec((1, modes), lambda s: (0, 0)),
            pl.BlockSpec((1, owners), lambda s: (0, 0)),
            pl.BlockSpec((1, place.size), lambda s: (0, 0)),
        ],
        out_specs=pl.BlockSpec((1, *shape[1:]), lambda s: (s, 0, 0, 0)),
        out_shape=jax.ShapeDtypeStruct(shape, jnp.bfloat16),
    )


def regroup(array, axis):
    shape = array.shape
    split = shape[:axis] + (2, QUARTERS, HALF) + shape[axis + 1 :]
    return jnp.swapaxes(array.reshape(split), axis, axis + 1).reshape(shape)


def complex_block(mix_weight):
    top_half = jnp.concatenate([mix_weight[0], mix_weight[1]], axis=1)
    bottom_half = jnp.concatenate([-mix_weight[1], mix_weight[0]], axis=1)
    return jnp.concatenate([top_half, bottom_half], axis=0)


def exchange(array, axes):
    flat = array.reshape(array.shape[0], -1, LANES)
    flat = lax.all_to_all(flat, axes, split_axis=0, concat_axis=0, tiled=True)
    return flat.reshape(array.shape)


def shards(fields, spectral_gain, mix_weight, column_list, column_counts):
    band_rows, lon_cols, channels = fields.shape
    lat_devices = lax.axis_size("lat")
    lon_devices = lax.axis_size("lon")
    owners = lat_devices * lon_devices
    lat_total = band_rows * lat_devices
    lon_total = lon_cols * lon_devices
    degrees = spectral_gain.shape[0]
    mode_count = column_list.shape[0]

    run_ends = jnp.cumsum(column_counts)
    starts = run_ends - column_counts
    offsets = jnp.arange(SLOTS, dtype=jnp.int32)
    positions = jnp.minimum(starts[None, :] + offsets[:, None], mode_count - 1)
    matches = positions[:, :, None] == jnp.arange(mode_count, dtype=jnp.int32)
    slot_orders = jnp.sum(jnp.where(matches, column_list, 0), axis=2)
    owner_index = lax.axis_index(("lat", "lon"))
    own_orders = lax.dynamic_slice_in_dim(slot_orders, owner_index, 1, axis=1)[:, 0]
    padded = jnp.arange(ROWS, dtype=jnp.int32)
    band, inside = padded // (ROWS // lat_devices), padded % (ROWS // lat_devices)
    row = (band * band_rows + jnp.minimum(inside, band_rows - 1)).astype(jnp.float32)
    colatitude = math.pi * (row + 0.5) / lat_total

    group = lax.axis_index("lon") // QUARTERS
    mine = jnp.arange(UNITS * UNIT, dtype=jnp.int32) + group * (UNITS * UNIT)
    mine = (lax.axis_index("lat") * band_rows + mine).astype(jnp.float32)
    weights = math.pi / lat_total * jnp.sin(math.pi * (mine + 0.5) / lat_total)
    weights = jnp.repeat(weights.reshape(UNITS, 1, UNIT), HALF, axis=2)
    gain = spectral_gain.reshape(degrees, 2 * channels)
    mixing = regroup(regroup(complex_block(mix_weight), 0), 1)

    def fourier(slots, after=()):
        return fourier_table(column_list, column_counts, slots, lon_devices, lon_cols, after)

    def turned(table, slots):
        factor = jnp.where(slot_orders[slice(*slots)] == 0, 1.0, 2.0).astype(jnp.bfloat16)
        return (table * factor[:, None, :, None]).reshape(-1, lon_devices * LON_PAD).T

    early, late = SLOT_CHUNKS
    early_table = fourier(early)
    gathered = exchange(pack(fields, (early_table, weights)), "lon")
    send = forward(gathered, early_table, weights, early)
    early_arrived = exchange(send, ("lat", "lon"))
    late_table = fourier(late, (send,))
    send = forward(gathered, late_table, weights, late)
    late_arrived = exchange(send, ("lat", "lon"))
    associated = legendre(own_orders, colatitude, degrees, (send,))
    early_back, late_back = turned(early_table, early), turned(late_table, late)
    early_spectrum, send = middle(
        early_arrived, associated, gain, mixing, early, (early_back, late_back)
    )
    early_landed = exchange(send, ("lat", "lon"))
    late_spectrum, send = middle(late_arrived, associated, gain, mixing, late)
    late_landed = exchange(send, ("lat", "lon"))
    spectrum = jnp.concatenate([early_spectrum, late_spectrum])
    partials = [inverse(early_landed, early_back, chunk, lon_total) for chunk in HOME_CHUNKS]
    spectrum = spectrum.reshape(1, SLOTS, degrees, 2, channels)
    sends = [
        inverse(late_landed, late_back, chunk, lon_total, partial, (spectrum,))
        for chunk, partial in zip(HOME_CHUNKS, partials)
    ]
    homes = [exchange(send, "lon") for send in sends]
    blended = None
    for chunk, home in zip(HOME_CHUNKS, homes):
        blended = blend(home, fields, chunk, blended)
    return blended, spectrum


def solution(mesh):
    placed = (P("lat", "lon", None), P(), P(), P(), P())
    return jax.shard_map(
        shards,
        mesh=mesh,
        in_specs=placed,
        out_specs=(P("lat", "lon", None), P(("lat", "lon"), None, None, None, None)),
        check_vma=False,
    )
```
